32 devices in a mesh: groups: 2 (over y), gs: 16 (over z, x, core).
Axes of the slice: x: 2, y: 2, z: 4, core: 2. Of those that a mesh axis runs over, the one named last changes fastest.
Arguments:
- params: float32 [59, 131072], P(None, ('groups', 'gs')), parts along dimension 1, may hold values from -620 to 620, as said below
- requests: int32 [512, 256], P(('groups', 'gs')), parts along dimension 0, may hold values from 0 to 4095, as said below
- member: int32 [512, 256], P(('groups', 'gs')), parts along dimension 0, may hold values from 0 to 4095, as said below
- tile_len: int32 [512], P(('groups', 'gs')), parts along dimension 0, may hold values from 1 to 256, 32768 in all
- tile_pos: int32 [512], P(('groups', 'gs')), parts along dimension 0, may hold values from 0 to 32399, as said below
- cam_shift: float32 [3, 16], P(None, 'groups'), parts along dimension 1, may hold values from -20 to 20
- pixel_grad: float32 [512, 3, 256], P(('groups', 'gs')), parts along dimension 0, may hold values from -6 to 6
Outputs:
- image: float32 [512, 3, 256], P(('groups', 'gs')), parts along dimension 0
- grad_params: float32 [59, 131072], P(None, ('groups', 'gs')), parts along dimension 1
The draws below stay inside these ranges and needn't reach their ends.
There are 2 independent parts, one for each index of `groups`. The reference program is written for one: setup_inputs(seed, part) draws one part's arguments, and reference() takes and returns one part's arrays. A program takes and returns all parts, laid end to end along the dimension named above; each array names one. Nothing has to cross between parts.
Inputs may be any that keep to these rules, and one draw needn't show every extreme that they name: `params`: rows 0 and 1 lie in -620 to 620, row 2 in 180 to 620, rows 3 to 5 in log 0.12 to log 0.9, row 6 in 1 to 2, rows 7 to 9 in -3 to 3, row 10 in -6 to 8, the rest in -1.5 to 1.5. `requests`: for each owner q, the rows r * 16 + q over all renderers r name each of its 4096 Gaussians exactly once. `member`: the 16 lists of one renderer name each of its 4096 slots exactly once. `tile_pos`: the tiles of one view are distinct.
All inputs are finite; a program needn't handle non-finite values. No bound on the sum of `tile_len` on one device may be relied on, other than what follows from the above.
Results may differ from the reference program's by a relative error of at most 0.0024.
Values sent between devices are 32-bit elements; how exact they have to be, the bound alone decides.
No kernel may reach another device: no remote copies, remote signals or barrier semaphores. Data moves between devices by JAX's collectives and lax.ppermute only.
A program may use at most 128 MiB of HBM per device.

```python
import math
import jax
import jax.numpy as jnp
import numpy as np
from jax import lax

PIXELS = 256
LIST = 256
VIEWS = 8
TILE_DEV = 16
G_DEV = 4096
CAP = 256
GAUSS = 65536
TILES = 256
N_GS = 16


def layout(key):
    owner_keys = jax.random.split(jax.random.fold_in(key, 101), N_GS)
    owner_order = jax.vmap(lambda subkey: jax.random.permutation(subkey, G_DEV))(owner_keys).astype(jnp.int32)
    slot_keys = jax.random.split(jax.random.fold_in(key, 102), N_GS)
    slot_order = jax.vmap(lambda subkey: jax.random.permutation(subkey, N_GS * CAP))(slot_keys).astype(jnp.int32)
    view_keys = jax.random.split(jax.random.fold_in(key, 103), VIEWS)
    view_tiles = jax.vmap(lambda subkey: jax.random.permutation(subkey, 32400))(view_keys).astype(jnp.int32)
    return (owner_order, slot_order, view_tiles)


def cameras(key):
    return jax.random.uniform(jax.random.fold_in(key, 104), (3, VIEWS), jnp.float32, -20.0, 20.0)


def tile_spots(view_tiles):
    flat = jnp.arange(N_GS * TILE_DEV, dtype=jnp.int32)
    renderer = flat // TILE_DEV
    within = renderer // VIEWS * TILE_DEV + flat % TILE_DEV
    return view_tiles[renderer % VIEWS, within]


def draw_requests(key, part):
    owner_order, slot_order, view_tiles = layout(key)
    arranged = jnp.transpose(owner_order.reshape(N_GS, N_GS, CAP), (1, 0, 2))
    return arranged.reshape(N_GS * N_GS, CAP).astype(jnp.int32)


def draw_member(key, part):
    owner_order, slot_order, view_tiles = layout(key)
    return slot_order.reshape(N_GS * TILE_DEV, LIST).astype(jnp.int32)


def draw_tile_pos(key, part):
    owner_order, slot_order, view_tiles = layout(key)
    return tile_spots(view_tiles).astype(jnp.int32)


def draw_cam_shift(key, part):
    return cameras(key)


def draw_params(key, part):
    owner_order, slot_order, view_tiles = layout(key)
    shifts = cameras(key)
    key = jax.random.fold_in(key, 11)
    keys = jax.random.split(key, 8)
    count = GAUSS
    position = jnp.argsort(owner_order, axis=1, stable=True).astype(jnp.int32)
    renderer = position // CAP
    slot_index = jnp.arange(N_GS, dtype=jnp.int32)[:, None] * CAP + position % CAP
    inverse = jnp.argsort(slot_order, axis=1, stable=True).astype(jnp.int32)
    placing = inverse[renderer, slot_index]
    tile_index = (renderer * TILE_DEV + placing // LIST).reshape(-1)
    entry = (placing % LIST).reshape(-1)
    view_index = (renderer % VIEWS).reshape(-1)
    spots_all = tile_spots(view_tiles)[tile_index]
    across = jax.random.uniform(keys[0], (count,), jnp.float32, 0.0, 1.0)
    down_frac = jax.random.uniform(keys[1], (count,), jnp.float32, 0.0, 1.0)
    deep_frac = jax.random.uniform(keys[2], (count,), jnp.float32, 0.0, 1.0)
    column = 16.0 * (spots_all % 240).astype(jnp.float32) + 16.0 * across
    row_place = 16.0 * (spots_all // 240).astype(jnp.float32) + 16.0 * down_frac
    u_home = column / 1920.0 - 1.0
    v_home = row_place / 1920.0 - 0.5625
    depth = 200.0 + 400.0 * (entry.astype(jnp.float32) + deep_frac) / LIST
    camera = shifts[:, view_index]
    planar = jnp.stack([camera[0] + u_home * depth, camera[1] + v_home * depth, camera[2] + depth])
    logscale = jax.random.uniform(keys[3], (3, count), jnp.float32, math.log(0.12), math.log(0.9))
    real_part = jax.random.uniform(keys[4], (1, count), jnp.float32, 1.0, 2.0)
    vector_part = jnp.clip(jax.random.normal(keys[5], (3, count), jnp.float32), -3.0, 3.0)
    opacity = -6.0 + 14.0 * jax.random.uniform(keys[6], (1, count), jnp.float32, 0.0, 1.0) ** 8
    coefs = jnp.clip(0.3 * jax.random.normal(keys[7], (48, count), jnp.float32), -1.5, 1.5)
    return jnp.concatenate([planar, logscale, real_part, vector_part, opacity, coefs], axis=0)


def shard_levels(stream_key, dims, cuts, low, high):
    factor_of, own = 1.0, jax.random.fold_in(stream_key, 6)
    for dim, blocks in cuts:
        steps = jnp.exp(jax.random.uniform(jax.random.fold_in(own, dim), (blocks,), jnp.float32, low / len(cuts), high / len(cuts)))
        factor_of = factor_of * jnp.repeat(steps, dims[dim] // blocks).reshape([-1 if axis == dim else 1 for axis in range(len(dims))])
    return factor_of


def profile(number_of, total, limit, skew):
    weights = [(1 << 20) // math.isqrt(standing ** skew) + 1 for standing in range(2, number_of + 1)]
    surplus, holding = total - limit - (number_of - 1), [1] * (number_of - 1)
    while surplus > 0:
        free = [i for i in range(number_of - 1) if holding[i] < limit]
        pool, left = sum([weights[i] for i in free]), surplus
        for i in free:
            addition = min(limit - holding[i], max(1, left * weights[i] // pool), surplus)
            holding[i] = holding[i] + addition
            surplus = surplus - addition
    return np.array([limit] + holding)


def uneven_parts(own_key, amount, total, limit, lean):
    if amount == 2:
        one = jax.random.randint(own_key, (), max(1, total - limit), min(limit, total - 1) + 1)
        return jnp.stack([one, total - one])
    lengths = jnp.asarray(profile(amount, total, limit, lean), jnp.int32)
    couples = (amount - 1) // 2
    donor, receiver = lengths[1:1 + 2 * couples:2], lengths[2:2 + 2 * couples:2]
    margin = jnp.minimum(donor - 1, limit - receiver)
    shifted = jax.random.randint(jax.random.fold_in(own_key, 1), (couples,), 0, 1 << 20) % (margin + 1)
    lengths = lengths.at[1:1 + 2 * couples:2].set(donor - shifted).at[2:2 + 2 * couples:2].set(receiver + shifted)
    return lengths[jax.random.permutation(jax.random.fold_in(own_key, 2), amount)]


def gaussian(stream_key, dims, scale, reach, pieces=(), kind=jnp.bfloat16):
    values = jax.random.normal(stream_key, dims, jnp.float32) * scale
    if len(pieces) > 0:
        values = shard_levels(stream_key, dims, pieces, -0.22, 0.18) * values
    return jnp.clip(values, min=-reach, max=reach).astype(kind)


def setup_inputs(seed: int = 0, part: int = 0) -> dict:
    key_list = jax.random.split(jax.random.key(seed), 8)
    part_splits = jax.random.split(jax.random.fold_in(key_list[7], part), 8)
    return {
        "params": draw_params(jax.random.fold_in(jax.random.fold_in(key_list[7], part), 71), part),
        "requests": draw_requests(jax.random.fold_in(jax.random.fold_in(key_list[7], part), 71), part),
        "member": draw_member(jax.random.fold_in(jax.random.fold_in(key_list[7], part), 71), part),
        "tile_len": uneven_parts(part_splits[3], TILES, TILES * LIST // 2, LIST, 2).astype(jnp.int32),
        "tile_pos": draw_tile_pos(jax.random.fold_in(jax.random.fold_in(key_list[7], part), 71), part),
        "cam_shift": draw_cam_shift(jax.random.fold_in(jax.random.fold_in(key_list[7], part), 71), part),
        "pixel_grad": gaussian(part_splits[6], (TILES, 3, PIXELS), 1.0, 6.0, ((0, 16),), jnp.float32),
    }


sh_c0 = 0.28209479177387814
sh_c1 = 0.4886025119029199
sh_c2 = (1.0925484305920792, -1.0925484305920792, 0.31539156525252005, -1.0925484305920792, 0.5462742152960396)
sh_c3 = (-0.5900435899266435, 2.890611442640554, -0.4570457994644658, 0.3731763325901154, -0.4570457994644658, 1.445305721320277, -0.5900435899266435)

def project(table, shift):
    xpos = table[0] - shift[0]
    ypos = table[1] - shift[1]
    zpos = table[2] - shift[2]
    scales = jnp.exp(table[3:6])
    quat = table[6:10] / jnp.sqrt(lax.optimization_barrier(jnp.sum(table[6:10] * table[6:10], axis=0)))
    qw, qx, qy, qz = (quat[0], quat[1], quat[2], quat[3])
    rot = [[1 - 2 * (qy * qy + qz * qz), 2 * (qx * qy - qw * qz), 2 * (qx * qz + qw * qy)], [2 * (qx * qy + qw * qz), 1 - 2 * (qx * qx + qz * qz), 2 * (qy * qz - qw * qx)], [2 * (qx * qz - qw * qy), 2 * (qy * qz + qw * qx), 1 - 2 * (qx * qx + qy * qy)]]
    first = [(rot[0][k] - xpos / zpos * rot[2][k]) * scales[k] / zpos for k in range(3)]
    second = [(rot[1][k] - ypos / zpos * rot[2][k]) * scales[k] / zpos for k in range(3)]
    cov_a = first[0] * first[0] + first[1] * first[1] + first[2] * first[2] + 8e-08
    cov_b = first[0] * second[0] + first[1] * second[1] + first[2] * second[2]
    cov_c = second[0] * second[0] + second[1] * second[1] + second[2] * second[2] + 8e-08
    determ = cov_a * cov_c - cov_b * cov_b
    length = jnp.sqrt(xpos * xpos + ypos * ypos + zpos * zpos)
    dx, dy, dz = (xpos / length, ypos / length, zpos / length)
    xx, yy, zz = (dx * dx, dy * dy, dz * dz)
    basis = jnp.stack([sh_c0 + 0.0 * dx, -sh_c1 * dy, sh_c1 * dz, -sh_c1 * dx, sh_c2[0] * dx * dy, sh_c2[1] * dy * dz, sh_c2[2] * (2 * zz - xx - yy), sh_c2[3] * dx * dz, sh_c2[4] * (xx - yy), sh_c3[0] * dy * (3 * xx - yy), sh_c3[1] * dx * dy * dz, sh_c3[2] * dy * (4 * zz - xx - yy), sh_c3[3] * dz * (2 * zz - 3 * xx - 3 * yy), sh_c3[4] * dx * (4 * zz - xx - yy), sh_c3[5] * dz * (xx - yy), sh_c3[6] * dx * (xx - 3 * yy)])
    colors = [jnp.maximum(0.5 + lax.optimization_barrier(jnp.sum(basis * table[11 + 16 * k:27 + 16 * k], axis=0)), 0.0) for k in range(3)]
    return jnp.stack([xpos / zpos, ypos / zpos, cov_c / determ, -cov_b / determ, cov_a / determ, jax.nn.sigmoid(table[10]), colors[0], colors[1], colors[2]])

def shade(selected_rows, length, position):
    count = selected_rows.shape[1]
    pixel = jnp.arange(256, dtype=jnp.int32)
    column = position % 240 * 16 + pixel % 16
    row_position = position // 240 * 16 + pixel // 16
    uval = (column.astype(jnp.float32) + 0.5) / 1920.0 - 1.0
    vertical_value = (row_position.astype(jnp.float32) + 0.5) / 1920.0 - 0.5625
    du = uval[None, :] - selected_rows[0][:, None]
    value_delta = vertical_value[None, :] - selected_rows[1][:, None]
    power = -0.5 * (selected_rows[2][:, None] * du * du + selected_rows[4][:, None] * value_delta * value_delta) - selected_rows[3][:, None] * du * value_delta
    alpha = jnp.minimum(0.99, selected_rows[5][:, None] * jnp.exp(power))
    order = jnp.arange(count, dtype=jnp.int32)
    alpha = jnp.where((order < length)[:, None], alpha, 0.0)
    lower = (order[:, None] > order[None, :]).astype(jnp.float32)
    prior_values = jnp.dot(lower, jnp.log1p(-alpha), precision=lax.Precision.HIGHEST)
    blend_weight = alpha * jnp.exp(prior_values)
    return jnp.dot(selected_rows[6:9], blend_weight, precision=lax.Precision.HIGHEST)

def shade_tiles(attrs, member, tile_len, tile_pos):
    selected_rows = jnp.moveaxis(jnp.take(attrs, member, axis=1), 1, 0)
    return jax.vmap(shade)(selected_rows, tile_len, tile_pos)

def reference(params, requests, member, tile_len, tile_pos, cam_shift, pixel_grad):

    def forward_render(table):

        @jax.checkpoint
        def one(renderer):
            asks = lax.dynamic_slice_in_dim(requests, renderer * N_GS, N_GS, 0)
            offsets = jnp.arange(N_GS, dtype=jnp.int32) * G_DEV
            glob = (asks + offsets[:, None]).reshape(-1).astype(jnp.int32)
            rows = jnp.take(table, glob, axis=1)
            shift = lax.dynamic_slice_in_dim(cam_shift, (renderer % VIEWS).astype(jnp.int32), 1, 1)
            attrs = project(rows, shift)
            start = (renderer * TILE_DEV).astype(jnp.int32)
            members = lax.dynamic_slice_in_dim(member, start, TILE_DEV, 0)
            lens = lax.dynamic_slice_in_dim(tile_len, start, TILE_DEV, 0)
            places = lax.dynamic_slice_in_dim(tile_pos, start, TILE_DEV, 0)
            return shade_tiles(attrs, members, lens, places)
        out = lax.map(one, jnp.arange(N_GS, dtype=jnp.int32))
        return out.reshape(TILES, 3, PIXELS)
    image, back = jax.vjp(forward_render, params)
    grad_params, = back(pixel_grad)
    return (image, grad_params)
```

```python
import functools

import jax
import jax.numpy as jnp
from jax import lax
from jax.experimental import pallas as pl
from jax.experimental.pallas import tpu as pltpu
from jax.sharding import PartitionSpec as P

f32, bf16, i32 = jnp.float32, jnp.bfloat16, jnp.int32

WIDE = 256
ATTRS = 9
SIDE = 16
ACROSS = 240
SCALE = 1920.0
LOG2E = 1.4426950408889634
FAR = -1.0e9

sh_c0 = 0.28209479177387814
sh_c1 = 0.4886025119029199
sh_c2 = (
    1.0925484305920792,
    -1.0925484305920792,
    0.31539156525252005,
    -1.0925484305920792,
    0.5462742152960396,
)
sh_c3 = (
    -0.5900435899266435,
    2.890611442640554,
    -0.4570457994644658,
    0.3731763325901154,
    -0.4570457994644658,
    1.445305721320277,
    -0.5900435899266435,
)


def project(table, shift):
    xpos = table[0] - shift[0]
    ypos = table[1] - shift[1]
    zpos = table[2] - shift[2]
    scales = [jnp.exp(table[3 + k]) for k in range(3)]
    quat = table[6:10]
    norm = 1.0 / jnp.sqrt(sum(part * part for part in quat))
    qw, qx, qy, qz = (part * norm for part in quat)
    rot = [
        [1 - 2 * (qy * qy + qz * qz), 2 * (qx * qy - qw * qz), 2 * (qx * qz + qw * qy)],
        [2 * (qx * qy + qw * qz), 1 - 2 * (qx * qx + qz * qz), 2 * (qy * qz - qw * qx)],
        [2 * (qx * qz - qw * qy), 2 * (qy * qz + qw * qx), 1 - 2 * (qx * qx + qy * qy)],
    ]
    inverse_z = 1.0 / zpos
    mean_u = xpos * inverse_z
    mean_v = ypos * inverse_z
    stretch = [scale * inverse_z for scale in scales]
    first = [(rot[0][k] - mean_u * rot[2][k]) * stretch[k] for k in range(3)]
    second = [(rot[1][k] - mean_v * rot[2][k]) * stretch[k] for k in range(3)]
    cov_a = first[0] * first[0] + first[1] * first[1] + first[2] * first[2] + 8e-08
    cov_b = first[0] * second[0] + first[1] * second[1] + first[2] * second[2]
    cov_c = second[0] * second[0] + second[1] * second[1] + second[2] * second[2] + 8e-08
    over_det = 1.0 / (cov_a * cov_c - cov_b * cov_b)
    over_length = 1.0 / jnp.sqrt(xpos * xpos + ypos * ypos + zpos * zpos)
    dx, dy, dz = (xpos * over_length, ypos * over_length, zpos * over_length)
    xx, yy, zz = (dx * dx, dy * dy, dz * dz)
    basis = [
        -sh_c1 * dy,
        sh_c1 * dz,
        -sh_c1 * dx,
        sh_c2[0] * dx * dy,
        sh_c2[1] * dy * dz,
        sh_c2[2] * (2 * zz - xx - yy),
        sh_c2[3] * dx * dz,
        sh_c2[4] * (xx - yy),
        sh_c3[0] * dy * (3 * xx - yy),
        sh_c3[1] * dx * dy * dz,
        sh_c3[2] * dy * (4 * zz - xx - yy),
        sh_c3[3] * dz * (2 * zz - 3 * xx - 3 * yy),
        sh_c3[4] * dx * (4 * zz - xx - yy),
        sh_c3[5] * dz * (xx - yy),
        sh_c3[6] * dx * (xx - 3 * yy),
    ]
    colors = []
    for k in range(3):
        total = 0.5 + sh_c0 * table[11 + 16 * k]
        for j, part in enumerate(basis):
            total = total + part * table[12 + 16 * k + j]
        colors.append(jnp.maximum(total, 0.0))
    opacity = 1.0 / (1.0 + jnp.exp(-table[10]))
    return [
        mean_u,
        mean_v,
        cov_c * over_det,
        -cov_b * over_det,
        cov_a * over_det,
        opacity,
        colors[0],
        colors[1],
        colors[2],
    ]


def pieces(value, count):
    out = []
    for left in range(count - 1, -1, -1):
        part = value.astype(bf16)
        out.append(part)
        if left:
            value = value - part.astype(f32)
    return out


def dot(one, other):
    return jnp.dot(one, other, preferred_element_type=f32)


def dot_nt(one, other):
    return lax.dot_general(one, other, (((1,), (1,)), ((), ())), preferred_element_type=f32)


def one_hot(low_row):
    rows = lax.broadcasted_iota(i32, (WIDE, WIDE), 0)
    return jnp.where(rows == low_row, 1.0, 0.0).astype(bf16)


def get(ref, start, count, stride=1, many=WIDE):
    rows = pl.ds(start, count, stride=stride) if stride > 1 else pl.ds(start, count)
    return jnp.concatenate([ref[h, rows, :] for h in range(many // 128)], axis=1)


def put(ref, start, count, value, stride=1):
    rows = pl.ds(start, count, stride=stride) if stride > 1 else pl.ds(start, count)
    for h in range(value.shape[1] // 128):
        ref[h, rows, :] = value[:, 128 * h : 128 * h + 128]


def invert(index_ref, inverse_ref):
    blocks = index_ref.shape[0]
    high_rows = lax.broadcasted_iota(i32, (blocks, WIDE), 0)
    lanes = lax.broadcasted_iota(i32, (blocks, WIDE), 1).astype(f32)
    total = jnp.zeros((2 * blocks, WIDE), f32)
    for j in range(blocks):
        row = index_ref[j : j + 1, :]
        here = high_rows == lax.shift_right_logical(row, 8)
        left = jnp.concatenate([jnp.where(here, float(j), 0.0), jnp.where(here, lanes, 0.0)], axis=0)
        total = total + dot_nt(left.astype(bf16), one_hot(row & (WIDE - 1)))
    found = total[:blocks] * float(WIDE) + total[blocks:]
    inverse_ref[...] = found.astype(i32)


def permute(held_ref, index_ref, count, give):
    blocks = index_ref.shape[0]
    parts = pieces(get(held_ref, 0, ATTRS * blocks), count)
    high_rows = lax.broadcasted_iota(i32, (blocks, WIDE), 0)
    for j in range(blocks):
        row = index_ref[j : j + 1, :]
        spread = one_hot(row & (WIDE - 1))
        high = lax.shift_right_logical(row, 8)
        found = dot(parts[0], spread)
        for part in parts[1:]:
            found = found + dot(part, spread)
        high_eight = jnp.broadcast_to(high, (8, WIDE))
        eight = found[0:8]
        for b in range(1, blocks):
            eight = jnp.where(high_eight == b, found[8 * b : 8 * b + 8], eight)
        ninth = jnp.sum(jnp.where(high_rows == high, found[8 * blocks :], 0.0), axis=0, keepdims=True)
        give(j, eight, ninth)


def put_travel(out_ref, blocks, packed, j, eight, ninth):
    for h in range(2):
        half = slice(128 * h, 128 * h + 128)
        if packed:
            out_ref[18 * j + 8 * h : 18 * j + 8 * h + 8, :] = eight[:, half]
            out_ref[18 * j + 16 + h : 18 * j + 17 + h, :] = ninth[:, half]
        else:
            out_ref[pl.ds(2 * j + h, 8, stride=2 * blocks), :] = eight[:, half]
            out_ref[16 * blocks + 2 * j + h : 16 * blocks + 2 * j + h + 1, :] = ninth[:, half]


def take_travel(in_ref, held_ref, blocks, packed):
    for j in range(blocks):
        for h in range(2):
            if packed:
                held_ref[h, 8 * j : 8 * j + 8, :] = in_ref[18 * j + 8 * h : 18 * j + 8 * h + 8, :]
                held_ref[h, 8 * blocks + j : 8 * blocks + j + 1, :] = in_ref[18 * j + 16 + h : 18 * j + 17 + h, :]
            else:
                held_ref[h, 8 * j : 8 * j + 8, :] = in_ref[pl.ds(2 * j + h, 8, stride=2 * blocks), :]
                held_ref[h, 8 * blocks + j : 8 * blocks + j + 1, :] = in_ref[
                    16 * blocks + 2 * j + h : 16 * blocks + 2 * j + h + 1, :
                ]


def prepare_kernel(params_ref, member_ref, grad_ref, dense_ref, inverse_ref, light_ref, turned_ref, light):
    width, count = params_ref.shape
    blocks = count // WIDE
    for first in range(0, width, 8):
        rows = min(8, width - first)
        for j in range(blocks):
            value = params_ref[first : first + rows, WIDE * j : WIDE * (j + 1)]
            put(dense_ref, first * blocks + j, rows, value, blocks)
    invert(member_ref, inverse_ref)
    tiles = grad_ref.shape[0]
    light[...] = jnp.zeros_like(light)
    for t in range(tiles):
        high, low = pieces(grad_ref[t], 2)
        light[16 * t : 16 * t + 3, :] = high.astype(f32)
        light[16 * t + 3 : 16 * t + 6, :] = low.astype(f32)
        light[16 * t + 6 : 16 * t + 9, :] = high.astype(f32)
    light_ref[...] = light[...].astype(bf16)
    for t in range(tiles):
        turned_ref[t] = light[16 * t : 16 * t + 16, :].T.astype(bf16)


def shifts(inverse, slots_per, cam_ref):
    views = cam_ref.shape[1]
    view = lax.rem(lax.div(inverse, slots_per), views)
    out = []
    for axis in range(3):
        value = jnp.full(inverse.shape, cam_ref[axis, 0], f32)
        for k in range(1, views):
            value = jnp.where(view == k, cam_ref[axis, k], value)
        out.append(value)
    return out


def dense_rows(ref, count, blocks):
    return [get(ref, k * blocks, blocks) for k in range(count)]


def owner_kernel(slots_per, packed, asked_ref, dense_ref, cam_ref, attrs_ref, inverse_ref, held):
    blocks = asked_ref.shape[0]
    width = dense_ref.shape[1] // blocks
    invert(asked_ref, inverse_ref)
    shift = shifts(inverse_ref[...], slots_per, cam_ref)
    attrs = project(dense_rows(dense_ref, width, blocks), shift)
    for a in range(8):
        put(held, a, blocks, attrs[a], 8)
    put(held, 8 * blocks, blocks, attrs[8])
    permute(held, asked_ref, 3, functools.partial(put_travel, attrs_ref, blocks, packed))


def return_kernel(slots_per, packed, back_ref, inverse_ref, dense_ref, cam_ref, out_ref, held, flat, grads):
    blocks = inverse_ref.shape[0]
    width = dense_ref.shape[1] // blocks
    take_travel(back_ref, held, blocks, packed)

    def give(j, eight, ninth):
        put(flat, j, 8, eight, blocks)
        put(flat, 8 * blocks + j, 1, ninth)

    permute(held, inverse_ref, 2, give)
    shift = shifts(inverse_ref[...], slots_per, cam_ref)
    _, back = jax.vjp(lambda rows: project(rows, shift), dense_rows(dense_ref, width, blocks))
    (rows,) = back(dense_rows(flat, ATTRS, blocks))
    for k in range(width):
        put(grads, k * blocks, blocks, rows[k])
    for first in range(0, width, 8):
        count = min(8, width - first)
        for j in range(blocks):
            value = get(grads, first * blocks + j, count, blocks)
            out_ref[first : first + count, WIDE * j : WIDE * (j + 1)] = value


def spread_scalars(values, tiles):
    rows = lax.broadcasted_iota(i32, (tiles, WIDE), 0)
    out = jnp.full((tiles, WIDE), values[0], values[0].dtype)
    for t in range(1, tiles):
        out = jnp.where(rows == t, values[t], out)
    return out


def offsets(index):
    column = lax.rem(index, SIDE).astype(f32) - (SIDE - 1) / 2
    row = lax.div(index, SIDE).astype(f32) - (SIDE - 1) / 2
    return column, row


def pick(index, choices):
    out = jnp.zeros(index.shape, f32)
    for k, choice in enumerate(choices):
        out = jnp.where(index == k, choice, out)
    return out


def render_kernel(
    packed,
    arrived_ref,
    member_ref,
    inverse_ref,
    light_ref,
    turned_ref,
    length_ref,
    place_ref,
    image_ref,
    back_ref,
    held,
    flat,
    coefs,
    sums,
    upper,
    lower,
    monomials,
    moments,
):
    tiles = member_ref.shape[0]
    blocks = tiles

    take_travel(arrived_ref, held, blocks, packed)

    def give(j, eight, ninth):
        put(flat, j, 8, eight, blocks)
        put(flat, 8 * blocks + j, 1, ninth)

    permute(held, member_ref, 3, give)

    mu, nu, con_a, con_b, con_c, opacity, *colors = dense_rows(flat, ATTRS, blocks)
    across = [lax.rem(place_ref[t], ACROSS).astype(f32) for t in range(tiles)]
    down = [lax.div(place_ref[t], ACROSS).astype(f32) for t in range(tiles)]
    centre_u = spread_scalars([(x * SIDE + SIDE / 2) / SCALE - 1.0 for x in across], tiles)
    centre_v = spread_scalars([(y * SIDE + SIDE / 2) / SCALE - 0.5625 for y in down], tiles)
    lengths = spread_scalars([length_ref[t] for t in range(tiles)], tiles)
    live = lax.broadcasted_iota(i32, (tiles, WIDE), 1) < lengths
    m = (mu - centre_u) * SCALE
    n = (nu - centre_v) * SCALE
    unit = LOG2E / (SCALE * SCALE)
    a = con_a * (-0.5 * unit)
    b = con_b * -unit
    c = con_c * (-0.5 * unit)
    lift = -2.0 * a * m - b * n
    tilt = -2.0 * c * n - b * m
    rest = -0.5 * (lift * m + tilt * n) + jnp.log2(opacity)
    terms = [a, b, c, lift, tilt]
    terms = [jnp.where(live, term, 0.0) for term in terms] + [jnp.where(live, rest, FAR)]
    coefs[...] = jnp.zeros_like(coefs)
    for k, term in enumerate(terms):
        for s, part in enumerate(pieces(term, 3)):
            row = 6 * s + k
            put(coefs, row * tiles, tiles, part.astype(f32))
    for k, color in enumerate(colors):
        high, low = (part.astype(f32) for part in pieces(color, 2))
        for row, part in ((32 + k, high), (35 + k, high), (38 + k, low)):
            put(coefs, row * tiles, tiles, part)

    row_index = lax.broadcasted_iota(i32, (WIDE, WIDE), 0)
    lane_index = lax.broadcasted_iota(i32, (WIDE, WIDE), 1)
    upper[...] = jnp.where(row_index < lane_index, 1.0, 0.0).astype(bf16)
    lower[...] = jnp.where(row_index > lane_index, 1.0, 0.0).astype(bf16)
    column, row = offsets(lax.broadcasted_iota(i32, (WIDE, 32), 0))
    which = lax.broadcasted_iota(i32, (WIDE, 32), 1)
    which = jnp.where(which < 18, lax.rem(which, 6), 6)
    one = jnp.ones((WIDE, 32), f32)
    monomials[...] = pick(
        which, [column * column, column * row, row * row, column, row, one]
    ).astype(bf16)
    column, row = offsets(lax.broadcasted_iota(i32, (16, WIDE), 1))
    which = lax.broadcasted_iota(i32, (16, WIDE), 0)
    one = jnp.ones((16, WIDE), f32)
    moments[...] = pick(
        which, [column * column, column * row, row * row, column, row, one]
    ).astype(bf16)
    sums[...] = jnp.zeros_like(sums)

    def one_tile(t, many):
        block = pl.ds(pl.multiple_of(16 * t, 16), 16)
        coef = get(coefs, t, 32, tiles, many).astype(bf16)
        color = get(coefs, t + 32 * tiles, 16, tiles, many).astype(bf16)
        power = jnp.exp2(dot(monomials[...], coef))
        alpha = jnp.minimum(power, 0.99)
        keep = 1.0 - alpha
        high, low = pieces(jnp.log2(keep), 2)
        before = upper[:many, :many]
        through = jnp.exp2(dot(high, before) + dot(low, before))
        weight = alpha * through
        high, low = pieces(weight, 2)
        picture = dot_nt(color, high) + dot_nt(color, low)
        image_ref[t] = picture[0:3] + picture[6:9]
        tint = dot(light_ref[block, :], high) + dot(light_ref[block, :], low)
        pull = dot(turned_ref[t], color)
        high, low = pieces(pull * weight, 2)
        after = lower[:many, :many]
        behind = dot(high, after) + dot(low, after)
        slope = (pull * through - behind / keep) * alpha
        high, low = pieces(jnp.where(power < 0.99, slope, 0.0), 2)
        moment = dot(moments[...], high) + dot(moments[...], low)
        put(sums, pl.multiple_of(16 * t, 16), 8, moment[0:8])
        put(sums, pl.multiple_of(16 * t + 8, 8), 8, tint[0:8] + pltpu.roll(tint[0:8], 5, 0))

    def step(t, carry):
        short = length_ref[t] <= WIDE // 2

        @pl.when(short)
        def _():
            one_tile(t, WIDE // 2)

        @pl.when(jnp.logical_not(short))
        def _():
            one_tile(t, WIDE)

        return carry

    lax.fori_loop(0, tiles, step, 0)

    m_xx, m_xy, m_yy, m_x, m_y, m_one = [get(sums, k, tiles, 16) for k in range(6)]
    d_x = m_x - m * m_one
    d_y = m_y - n * m_one
    d_xx = m_xx - m * (m_x + d_x)
    d_xy = m_xy - m * m_y - n * d_x
    d_yy = m_yy - n * (m_y + d_y)
    shrink = 1.0 / SCALE
    grads = [
        (con_a * d_x + con_b * d_y) * shrink,
        (con_c * d_y + con_b * d_x) * shrink,
        d_xx * (-0.5 * shrink * shrink),
        d_xy * (-shrink * shrink),
        d_yy * (-0.5 * shrink * shrink),
        m_one / opacity,
        *[get(sums, 8 + k, tiles, 16) for k in range(3)],
    ]
    for k in range(8):
        put(held, k, blocks, grads[k], 8)
    put(held, 8 * blocks, blocks, grads[8])
    permute(held, inverse_ref, 2, functools.partial(put_travel, back_ref, blocks, packed))


def vmem(count):
    return [pl.BlockSpec(memory_space=pltpu.VMEM)] * count


def smem(count):
    return [pl.BlockSpec(memory_space=pltpu.SMEM)] * count


def shape(*dims, dtype=f32):
    return jax.ShapeDtypeStruct(dims, dtype)


def call(kernel, name, ins, outs, scratch, cycles):
    return pl.pallas_call(
        kernel,
        out_shape=outs,
        in_specs=ins,
        out_specs=vmem(len(outs)),
        scratch_shapes=scratch,
        name=name,
        compiler_params=pltpu.CompilerParams(vmem_limit_bytes=48 * 1024 * 1024),
        cost_estimate=pl.CostEstimate(flops=cycles, bytes_accessed=4_000_000, transcendentals=0),
    )


def travel(rows, peers, slots, packed):
    total = rows.shape[0]
    if packed:
        parts = rows.reshape(peers, 1, -1)
    else:
        parts = jnp.swapaxes(rows.reshape(ATTRS, peers, slots), 0, 1)
    parts = lax.all_to_all(parts, "gs", split_axis=0, concat_axis=0, tiled=True)
    if not packed:
        parts = jnp.swapaxes(parts, 0, 1)
    return parts.reshape(total, 128)


def on_device(params, requests, member, tile_len, tile_pos, cam_shift, pixel_grad):
    peers, slots = requests.shape
    width, count = params.shape
    tiles = member.shape[0]
    blocks = count // WIDE
    packed = slots % WIDE == 0
    held = pltpu.VMEM((2, ATTRS * blocks, 128), f32)
    rows = shape(18 * blocks, 128)
    index = shape(blocks, WIDE, dtype=i32)

    asked = lax.all_to_all(requests, "gs", split_axis=0, concat_axis=0, tiled=True)
    asked = asked.reshape(blocks, WIDE)
    dense, inverse, light, turned = call(
        prepare_kernel,
        "prepare",
        vmem(3),
        [
            shape(2, width * blocks, 128),
            index,
            shape(16 * tiles, WIDE, dtype=bf16),
            shape(tiles, WIDE, 16, dtype=bf16),
        ],
        [pltpu.VMEM((16 * tiles, WIDE), f32)],
        10_000_000,
    )(params, member, pixel_grad)
    attrs, place = call(
        functools.partial(owner_kernel, slots, packed),
        "owner",
        vmem(2) + smem(1),
        [rows, index],
        [held],
        10_000_000,
    )(asked, dense, cam_shift)
    arrived = travel(attrs, peers, slots, packed)
    image, back = call(
        functools.partial(render_kernel, packed),
        "render",
        vmem(5) + smem(2),
        [shape(tiles, 3, WIDE), rows],
        [
            held,
            held,
            pltpu.VMEM((2, 48 * tiles, 128), f32),
            pltpu.VMEM((2, 16 * tiles, 128), f32),
            pltpu.VMEM((WIDE, WIDE), bf16),
            pltpu.VMEM((WIDE, WIDE), bf16),
            pltpu.VMEM((WIDE, 32), bf16),
            pltpu.VMEM((16, WIDE), bf16),
        ],
        100_000_000,
    )(arrived, member, inverse, light, turned, tile_len, tile_pos)
    returned = travel(back, peers, slots, packed)
    (grad_params,) = call(
        functools.partial(return_kernel, slots, packed),
        "return",
        vmem(3) + smem(1),
        [shape(width, count)],
        [held, held, pltpu.VMEM((2, width * blocks, 128), f32)],
        10_000_000,
    )(returned, place, dense, cam_shift)
    return (image, grad_params)


def solution(mesh):
    return jax.shard_map(
        on_device,
        mesh=mesh,
        in_specs=(
            P(None, ("groups", "gs")),
            P(("groups", "gs"), None),
            P(("groups", "gs"), None),
            P(("groups", "gs")),
            P(("groups", "gs")),
            P(None, "groups"),
            P(("groups", "gs"), None, None),
        ),
        out_specs=(P(("groups", "gs"), None, None), P(None, ("groups", "gs"))),
        check_vma=False,
    )
```

```python
import functools

import jax
import jax.numpy as jnp
from jax import lax
from jax.experimental import pallas as pl
from jax.experimental.pallas import tpu as pltpu
from jax.sharding import PartitionSpec as P

f32, bf16, i32 = jnp.float32, jnp.bfloat16, jnp.int32

WIDE = 256
ATTRS = 9
SIDE = 16
ACROSS = 240
SCALE = 1920.0
LOG2E = 1.4426950408889634
GROUP = 2
FAR = -1.0e9

sh_c0 = 0.28209479177387814
sh_c1 = 0.4886025119029199
sh_c2 = (
    1.0925484305920792,
    -1.0925484305920792,
    0.31539156525252005,
    -1.0925484305920792,
    0.5462742152960396,
)
sh_c3 = (
    -0.5900435899266435,
    2.890611442640554,
    -0.4570457994644658,
    0.3731763325901154,
    -0.4570457994644658,
    1.445305721320277,
    -0.5900435899266435,
)


def project(table, shift):
    xpos = table[0] - shift[0]
    ypos = table[1] - shift[1]
    zpos = table[2] - shift[2]
    scales = [jnp.exp(table[3 + k]) for k in range(3)]
    quat = table[6:10]
    norm = 1.0 / jnp.sqrt(sum(part * part for part in quat))
    qw, qx, qy, qz = (part * norm for part in quat)
    rot = [
        [1 - 2 * (qy * qy + qz * qz), 2 * (qx * qy - qw * qz), 2 * (qx * qz + qw * qy)],
        [2 * (qx * qy + qw * qz), 1 - 2 * (qx * qx + qz * qz), 2 * (qy * qz - qw * qx)],
        [2 * (qx * qz - qw * qy), 2 * (qy * qz + qw * qx), 1 - 2 * (qx * qx + qy * qy)],
    ]
    inverse_z = 1.0 / zpos
    mean_u = xpos * inverse_z
    mean_v = ypos * inverse_z
    stretch = [scale * inverse_z for scale in scales]
    first = [(rot[0][k] - mean_u * rot[2][k]) * stretch[k] for k in range(3)]
    second = [(rot[1][k] - mean_v * rot[2][k]) * stretch[k] for k in range(3)]
    cov_a = first[0] * first[0] + first[1] * first[1] + first[2] * first[2] + 8e-08
    cov_b = first[0] * second[0] + first[1] * second[1] + first[2] * second[2]
    cov_c = second[0] * second[0] + second[1] * second[1] + second[2] * second[2] + 8e-08
    over_det = 1.0 / (cov_a * cov_c - cov_b * cov_b)
    over_length = 1.0 / jnp.sqrt(xpos * xpos + ypos * ypos + zpos * zpos)
    dx, dy, dz = (xpos * over_length, ypos * over_length, zpos * over_length)
    xx, yy, zz = (dx * dx, dy * dy, dz * dz)
    basis = [
        -sh_c1 * dy,
        sh_c1 * dz,
        -sh_c1 * dx,
        sh_c2[0] * dx * dy,
        sh_c2[1] * dy * dz,
        sh_c2[2] * (2 * zz - xx - yy),
        sh_c2[3] * dx * dz,
        sh_c2[4] * (xx - yy),
        sh_c3[0] * dy * (3 * xx - yy),
        sh_c3[1] * dx * dy * dz,
        sh_c3[2] * dy * (4 * zz - xx - yy),
        sh_c3[3] * dz * (2 * zz - 3 * xx - 3 * yy),
        sh_c3[4] * dx * (4 * zz - xx - yy),
        sh_c3[5] * dz * (xx - yy),
        sh_c3[6] * dx * (xx - 3 * yy),
    ]
    colors = []
    for k in range(3):
        total = 0.5 + sh_c0 * table[11 + 16 * k]
        for j, part in enumerate(basis):
            total = total + part * table[12 + 16 * k + j]
        colors.append(jnp.maximum(total, 0.0))
    opacity = 1.0 / (1.0 + jnp.exp(-table[10]))
    return [
        mean_u,
        mean_v,
        cov_c * over_det,
        -cov_b * over_det,
        cov_a * over_det,
        opacity,
        colors[0],
        colors[1],
        colors[2],
    ]


def pieces(value, count):
    out = []
    for left in range(count - 1, -1, -1):
        part = value.astype(bf16)
        out.append(part)
        if left:
            value = value - part.astype(f32)
    return out


def dot(one, other):
    return jnp.dot(one, other, preferred_element_type=f32)


def dot_nt(one, other):
    return lax.dot_general(one, other, (((1,), (1,)), ((), ())), preferred_element_type=f32)


def one_hot(low_row):
    rows = lax.broadcasted_iota(i32, (WIDE, WIDE), 0)
    return jnp.where(rows == low_row, 1.0, 0.0).astype(bf16)


def get(ref, start, count, stride=1, many=WIDE):
    rows = pl.ds(start, count, stride=stride) if stride > 1 else pl.ds(start, count)
    return jnp.concatenate([ref[h, rows, :] for h in range(many // 128)], axis=1)


def put(ref, start, count, value, stride=1):
    rows = pl.ds(start, count, stride=stride) if stride > 1 else pl.ds(start, count)
    for h in range(value.shape[1] // 128):
        ref[h, rows, :] = value[:, 128 * h : 128 * h + 128]


def invert(index_ref, inverse_ref):
    blocks = index_ref.shape[0]
    high_rows = lax.broadcasted_iota(i32, (blocks, WIDE), 0)
    lanes = lax.broadcasted_iota(i32, (blocks, WIDE), 1).astype(f32)
    total = jnp.zeros((2 * blocks, WIDE), f32)
    for j in range(blocks):
        row = index_ref[j : j + 1, :]
        here = high_rows == lax.shift_right_logical(row, 8)
        left = jnp.concatenate([jnp.where(here, float(j), 0.0), jnp.where(here, lanes, 0.0)], axis=0)
        total = total + dot_nt(left.astype(bf16), one_hot(row & (WIDE - 1)))
    found = total[:blocks] * float(WIDE) + total[blocks:]
    inverse_ref[...] = found.astype(i32)


def permute(held_ref, index_ref, count, give):
    blocks = index_ref.shape[0]
    parts = pieces(get(held_ref, 0, ATTRS * blocks), count)
    high_rows = lax.broadcasted_iota(i32, (blocks, WIDE), 0)
    for j in range(blocks):
        row = index_ref[j : j + 1, :]
        spread = one_hot(row & (WIDE - 1))
        high = lax.shift_right_logical(row, 8)
        found = dot(parts[0], spread)
        for part in parts[1:]:
            found = found + dot(part, spread)
        high_eight = jnp.broadcast_to(high, (8, WIDE))
        eight = found[0:8]
        for b in range(1, blocks):
            eight = jnp.where(high_eight == b, found[8 * b : 8 * b + 8], eight)
        ninth = jnp.sum(jnp.where(high_rows == high, found[8 * blocks :], 0.0), axis=0, keepdims=True)
        give(j, eight, ninth)


def put_travel(out_ref, blocks, packed, j, eight, ninth):
    for h in range(2):
        half = slice(128 * h, 128 * h + 128)
        if packed:
            out_ref[18 * j + 8 * h : 18 * j + 8 * h + 8, :] = eight[:, half]
            out_ref[18 * j + 16 + h : 18 * j + 17 + h, :] = ninth[:, half]
        else:
            out_ref[pl.ds(2 * j + h, 8, stride=2 * blocks), :] = eight[:, half]
            out_ref[16 * blocks + 2 * j + h : 16 * blocks + 2 * j + h + 1, :] = ninth[:, half]


def take_travel(in_ref, held_ref, blocks, packed):
    for j in range(blocks):
        for h in range(2):
            if packed:
                held_ref[h, 8 * j : 8 * j + 8, :] = in_ref[18 * j + 8 * h : 18 * j + 8 * h + 8, :]
                held_ref[h, 8 * blocks + j : 8 * blocks + j + 1, :] = in_ref[18 * j + 16 + h : 18 * j + 17 + h, :]
            else:
                held_ref[h, 8 * j : 8 * j + 8, :] = in_ref[pl.ds(2 * j + h, 8, stride=2 * blocks), :]
                held_ref[h, 8 * blocks + j : 8 * blocks + j + 1, :] = in_ref[
                    16 * blocks + 2 * j + h : 16 * blocks + 2 * j + h + 1, :
                ]


def spread_scalars(values, tiles):
    rows = lax.broadcasted_iota(i32, (tiles, WIDE), 0)
    out = jnp.full((tiles, WIDE), values[0], values[0].dtype)
    for t in range(1, tiles):
        out = jnp.where(rows == t, values[t], out)
    return out


def prepare_kernel(
    params_ref,
    member_ref,
    grad_ref,
    length_ref,
    place_ref,
    cam_ref,
    dense_ref,
    inverse_ref,
    light_ref,
    turned_ref,
    centre_ref,
    camera_ref,
    plan_ref,
    light,
):
    width, count = params_ref.shape
    blocks = count // WIDE
    for first in range(0, width, 8):
        rows = min(8, width - first)
        for j in range(blocks):
            value = params_ref[first : first + rows, WIDE * j : WIDE * (j + 1)]
            put(dense_ref, first * blocks + j, rows, value, blocks)
    invert(member_ref, inverse_ref)
    tiles = grad_ref.shape[0]
    light[...] = jnp.zeros_like(light)
    for t in range(tiles):
        high, low = pieces(grad_ref[t], 2)
        light[16 * t : 16 * t + 3, :] = high.astype(f32)
        light[16 * t + 3 : 16 * t + 6, :] = low.astype(f32)
        light[16 * t + 6 : 16 * t + 9, :] = high.astype(f32)
    light_ref[...] = light[...].astype(bf16)
    for t in range(tiles):
        turned_ref[t] = light[16 * t : 16 * t + 16, :].T.astype(bf16)
    across = [lax.rem(place_ref[t], ACROSS).astype(f32) for t in range(tiles)]
    down = [lax.div(place_ref[t], ACROSS).astype(f32) for t in range(tiles)]
    centre_ref[0] = spread_scalars([(x * SIDE + SIDE / 2) / SCALE - 1.0 for x in across], tiles)
    centre_ref[1] = spread_scalars([(y * SIDE + SIDE / 2) / SCALE - 0.5625 for y in down], tiles)
    lengths = spread_scalars([length_ref[t] for t in range(tiles)], tiles)
    live = lax.broadcasted_iota(i32, (tiles, WIDE), 1) < lengths
    centre_ref[2] = jnp.where(live, 1.0, 0.0)
    views = cam_ref.shape[1]
    for axis in range(3):
        for k in range(views):
            row = axis * views + k
            camera_ref[row : row + 1, :] = jnp.full((1, WIDE), cam_ref[axis, k], f32)
    wide = [(length_ref[t] > WIDE // 2).astype(i32) for t in range(tiles)]
    many = sum(wide[1:], wide[0])
    first, last = jnp.int32(0), many
    for t in range(tiles):
        plan_ref[jnp.where(wide[t] > 0, first, last)] = t
        first, last = first + wide[t], last + 1 - wide[t]
    plan_ref[tiles] = lax.div(many + GROUP - 1, GROUP)


def shifts(inverse, slots_per, camera_ref):
    views = camera_ref.shape[0] // 3
    view = lax.rem(lax.div(inverse, slots_per), views)
    out = []
    for axis in range(3):
        rows = [camera_ref[axis * views + k : axis * views + k + 1, :] for k in range(views)]
        value = jnp.broadcast_to(rows[0], inverse.shape)
        for k in range(1, views):
            value = jnp.where(view == k, rows[k], value)
        out.append(value)
    return out


def dense_rows(ref, count, blocks):
    return [get(ref, k * blocks, blocks) for k in range(count)]


def owner_kernel(slots_per, packed, asked_ref, dense_ref, camera_ref, attrs_ref, inverse_ref, held):
    blocks = asked_ref.shape[0]
    width = dense_ref.shape[1] // blocks
    invert(asked_ref, inverse_ref)
    shift = shifts(inverse_ref[...], slots_per, camera_ref)
    attrs = project(dense_rows(dense_ref, width, blocks), shift)
    for a in range(8):
        put(held, a, blocks, attrs[a], 8)
    put(held, 8 * blocks, blocks, attrs[8])
    permute(held, asked_ref, 3, functools.partial(put_travel, attrs_ref, blocks, packed))


def return_kernel(slots_per, packed, back_ref, inverse_ref, dense_ref, camera_ref, out_ref, held, flat, grads):
    blocks = inverse_ref.shape[0]
    width = dense_ref.shape[1] // blocks
    take_travel(back_ref, held, blocks, packed)

    def give(j, eight, ninth):
        put(flat, j, 8, eight, blocks)
        put(flat, 8 * blocks + j, 1, ninth)

    permute(held, inverse_ref, 2, give)
    shift = shifts(inverse_ref[...], slots_per, camera_ref)
    _, back = jax.vjp(lambda rows: project(rows, shift), dense_rows(dense_ref, width, blocks))
    (rows,) = back(dense_rows(flat, ATTRS, blocks))
    for k in range(width):
        put(grads, k * blocks, blocks, rows[k])
    for first in range(0, width, 8):
        count = min(8, width - first)
        for j in range(blocks):
            value = get(grads, first * blocks + j, count, blocks)
            out_ref[first : first + count, WIDE * j : WIDE * (j + 1)] = value


def offsets(index):
    column = lax.rem(index, SIDE).astype(f32) - (SIDE - 1) / 2
    row = lax.div(index, SIDE).astype(f32) - (SIDE - 1) / 2
    return column, row


def pick(index, choices):
    out = jnp.zeros(index.shape, f32)
    for k, choice in enumerate(choices):
        out = jnp.where(index == k, choice, out)
    return out


def render_kernel(
    packed,
    arrived_ref,
    member_ref,
    inverse_ref,
    light_ref,
    turned_ref,
    centre_ref,
    plan_ref,
    image_ref,
    back_ref,
    held,
    flat,
    coefs,
    sums,
    upper,
    lower,
    monomials,
    moments,
):
    tiles = member_ref.shape[0]
    blocks = tiles

    take_travel(arrived_ref, held, blocks, packed)

    def give(j, eight, ninth):
        put(flat, j, 8, eight, blocks)
        put(flat, 8 * blocks + j, 1, ninth)

    permute(held, member_ref, 3, give)

    mu, nu, con_a, con_b, con_c, opacity, *colors = dense_rows(flat, ATTRS, blocks)
    centre_u, centre_v, live = (centre_ref[k] for k in range(3))
    live = live > 0.0
    m = (mu - centre_u) * SCALE
    n = (nu - centre_v) * SCALE
    unit = LOG2E / (SCALE * SCALE)
    a = con_a * (-0.5 * unit)
    b = con_b * -unit
    c = con_c * (-0.5 * unit)
    lift = -2.0 * a * m - b * n
    tilt = -2.0 * c * n - b * m
    rest = -0.5 * (lift * m + tilt * n) + jnp.log2(opacity)
    terms = [a, b, c, lift, tilt]
    terms = [jnp.where(live, term, 0.0) for term in terms] + [jnp.where(live, rest, FAR)]
    coefs[...] = jnp.zeros_like(coefs)
    for k, term in enumerate(terms):
        for s, part in enumerate(pieces(term, 3)):
            row = 6 * s + k
            put(coefs, row * tiles, tiles, part.astype(f32))
    for k, color in enumerate(colors):
        high, low = (part.astype(f32) for part in pieces(color, 2))
        for row, part in ((32 + k, high), (35 + k, high), (38 + k, low)):
            put(coefs, row * tiles, tiles, part)

    row_index = lax.broadcasted_iota(i32, (WIDE, WIDE), 0)
    lane_index = lax.broadcasted_iota(i32, (WIDE, WIDE), 1)
    upper[...] = jnp.where(row_index < lane_index, 1.0, 0.0).astype(bf16)
    lower[...] = jnp.where(row_index > lane_index, 1.0, 0.0).astype(bf16)
    column, row = offsets(lax.broadcasted_iota(i32, (WIDE, 32), 0))
    which = lax.broadcasted_iota(i32, (WIDE, 32), 1)
    which = jnp.where(which < 18, lax.rem(which, 6), 6)
    one = jnp.ones((WIDE, 32), f32)
    monomials[...] = pick(
        which, [column * column, column * row, row * row, column, row, one]
    ).astype(bf16)
    column, row = offsets(lax.broadcasted_iota(i32, (16, WIDE), 1))
    which = lax.broadcasted_iota(i32, (16, WIDE), 0)
    one = jnp.ones((16, WIDE), f32)
    moments[...] = pick(
        which, [column * column, column * row, row * row, column, row, one]
    ).astype(bf16)
    sums[...] = jnp.zeros_like(sums)

    def some_tiles(turn, many):
        ts = [plan_ref[GROUP * turn + k] for k in range(GROUP)]
        block = [pl.ds(pl.multiple_of(16 * t, 16), 16) for t in ts]
        coef = [get(coefs, t, 32, tiles, many).astype(bf16) for t in ts]
        color = [get(coefs, t + 32 * tiles, 16, tiles, many).astype(bf16) for t in ts]
        power = [jnp.exp2(dot(monomials[...], x)) for x in coef]
        alpha = [jnp.minimum(x, 0.99) for x in power]
        keep = [1.0 - x for x in alpha]
        parts = [pieces(jnp.log2(x), 2) for x in keep]
        before = upper[:many, :many]
        through = [jnp.exp2(dot(high, before) + dot(low, before)) for high, low in parts]
        pull = [dot(turned_ref[t], x) for t, x in zip(ts, color)]
        weight = [x * y for x, y in zip(alpha, through)]
        parts = [pieces(x * y, 2) for x, y in zip(pull, weight)]
        after = lower[:many, :many]
        behind = [dot(high, after) + dot(low, after) for high, low in parts]
        parts = [pieces(x, 2) for x in weight]
        for t, x, (high, low) in zip(ts, color, parts):
            picture = dot_nt(x, high) + dot_nt(x, low)
            image_ref[t] = picture[0:3] + picture[6:9]
        for t, rows, (high, low) in zip(ts, block, parts):
            tint = dot(light_ref[rows, :], high) + dot(light_ref[rows, :], low)
            put(sums, pl.multiple_of(16 * t + 8, 8), 8, tint[0:8] + pltpu.roll(tint[0:8], 5, 0))
        for k, t in enumerate(ts):
            slope = (pull[k] * through[k] - behind[k] / keep[k]) * alpha[k]
            high, low = pieces(jnp.where(power[k] < 0.99, slope, 0.0), 2)
            moment = dot(moments[...], high) + dot(moments[...], low)
            put(sums, pl.multiple_of(16 * t, 16), 8, moment[0:8])

    def wide_turn(turn, carry):
        some_tiles(turn, WIDE)
        return carry

    def narrow_turn(turn, carry):
        some_tiles(turn, WIDE // 2)
        return carry

    wide_turns = plan_ref[tiles]
    lax.fori_loop(0, wide_turns, wide_turn, 0)
    lax.fori_loop(wide_turns, tiles // GROUP, narrow_turn, 0)

    m_xx, m_xy, m_yy, m_x, m_y, m_one = [get(sums, k, tiles, 16) for k in range(6)]
    d_x = m_x - m * m_one
    d_y = m_y - n * m_one
    d_xx = m_xx - m * (m_x + d_x)
    d_xy = m_xy - m * m_y - n * d_x
    d_yy = m_yy - n * (m_y + d_y)
    shrink = 1.0 / SCALE
    grads = [
        (con_a * d_x + con_b * d_y) * shrink,
        (con_c * d_y + con_b * d_x) * shrink,
        d_xx * (-0.5 * shrink * shrink),
        d_xy * (-shrink * shrink),
        d_yy * (-0.5 * shrink * shrink),
        m_one / opacity,
        *[get(sums, 8 + k, tiles, 16) for k in range(3)],
    ]
    for k in range(8):
        put(held, k, blocks, grads[k], 8)
    put(held, 8 * blocks, blocks, grads[8])
    permute(held, inverse_ref, 2, functools.partial(put_travel, back_ref, blocks, packed))


def vmem(count):
    return [pl.BlockSpec(memory_space=pltpu.VMEM)] * count


def smem(count):
    return [pl.BlockSpec(memory_space=pltpu.SMEM)] * count


def shape(*dims, dtype=f32):
    return jax.ShapeDtypeStruct(dims, dtype)


def call(kernel, name, ins, outs, scratch, cycles, scalars=0):
    return pl.pallas_call(
        kernel,
        out_shape=outs,
        in_specs=ins,
        out_specs=vmem(len(outs) - scalars) + smem(scalars),
        scratch_shapes=scratch,
        name=name,
        compiler_params=pltpu.CompilerParams(vmem_limit_bytes=48 * 1024 * 1024),
        cost_estimate=pl.CostEstimate(flops=cycles, bytes_accessed=4_000_000, transcendentals=0),
    )


def travel(rows, peers, slots, packed):
    total = rows.shape[0]
    if packed:
        parts = rows.reshape(peers, 1, -1)
    else:
        parts = jnp.swapaxes(rows.reshape(ATTRS, peers, slots), 0, 1)
    parts = lax.all_to_all(parts, "gs", split_axis=0, concat_axis=0, tiled=True)
    if not packed:
        parts = jnp.swapaxes(parts, 0, 1)
    return parts.reshape(total, 128)


def on_device(params, requests, member, tile_len, tile_pos, cam_shift, pixel_grad):
    peers, slots = requests.shape
    width, count = params.shape
    tiles = member.shape[0]
    blocks = count // WIDE
    packed = slots % WIDE == 0
    held = pltpu.VMEM((2, ATTRS * blocks, 128), f32)
    rows = shape(18 * blocks, 128)
    index = shape(blocks, WIDE, dtype=i32)

    asked = lax.all_to_all(requests, "gs", split_axis=0, concat_axis=0, tiled=True)
    asked = asked.reshape(blocks, WIDE)
    dense, inverse, light, turned, centre, camera, plan = call(
        prepare_kernel,
        "prepare",
        vmem(3) + smem(3),
        [
            shape(2, width * blocks, 128),
            index,
            shape(16 * tiles, WIDE, dtype=bf16),
            shape(tiles, WIDE, 16, dtype=bf16),
            shape(3, tiles, WIDE),
            shape(3 * cam_shift.shape[1], WIDE),
            shape(tiles + 1, dtype=i32),
        ],
        [pltpu.VMEM((16 * tiles, WIDE), f32)],
        10_000_000,
        scalars=1,
    )(params, member, pixel_grad, tile_len, tile_pos, cam_shift)
    attrs, place = call(
        functools.partial(owner_kernel, slots, packed),
        "owner",
        vmem(3),
        [rows, index],
        [held],
        10_000_000,
    )(asked, dense, camera)
    arrived = travel(attrs, peers, slots, packed)
    image, back = call(
        functools.partial(render_kernel, packed),
        "render",
        vmem(6) + smem(1),
        [shape(tiles, 3, WIDE), rows],
        [
            held,
            held,
            pltpu.VMEM((2, 48 * tiles, 128), f32),
            pltpu.VMEM((2, 16 * tiles, 128), f32),
            pltpu.VMEM((WIDE, WIDE), bf16),
            pltpu.VMEM((WIDE, WIDE), bf16),
            pltpu.VMEM((WIDE, 32), bf16),
            pltpu.VMEM((16, WIDE), bf16),
        ],
        100_000_000,
    )(arrived, member, inverse, light, turned, centre, plan)
    returned = travel(back, peers, slots, packed)
    (grad_params,) = call(
        functools.partial(return_kernel, slots, packed),
        "return",
        vmem(4),
        [shape(width, count)],
        [held, held, pltpu.VMEM((2, width * blocks, 128), f32)],
        10_000_000,
    )(returned, place, dense, camera)
    return (image, grad_params)


def solution(mesh):
    return jax.shard_map(
        on_device,
        mesh=mesh,
        in_specs=(
            P(None, ("groups", "gs")),
            P(("groups", "gs"), None),
            P(("groups", "gs"), None),
            P(("groups", "gs")),
            P(("groups", "gs")),
            P(None, "groups"),
            P(("groups", "gs"), None, None),
        ),
        out_specs=(P(("groups", "gs"), None, None), P(None, ("groups", "gs"))),
        check_vma=False,
    )
```

```python
import functools

import jax
import jax.numpy as jnp
from jax import lax
from jax.experimental import pallas as pl
from jax.experimental.pallas import tpu as pltpu
from jax.sharding import PartitionSpec as P

f32, bf16, i32 = jnp.float32, jnp.bfloat16, jnp.int32

WIDE = 256
ATTRS = 9
SIDE = 16
ACROSS = 240
SCALE = 1920.0
LOG2E = 1.4426950408889634
GROUP = 4
FAR = -1.0e9

sh_c0 = 0.28209479177387814
sh_c1 = 0.4886025119029199
sh_c2 = (
    1.0925484305920792,
    -1.0925484305920792,
    0.31539156525252005,
    -1.0925484305920792,
    0.5462742152960396,
)
sh_c3 = (
    -0.5900435899266435,
    2.890611442640554,
    -0.4570457994644658,
    0.3731763325901154,
    -0.4570457994644658,
    1.445305721320277,
    -0.5900435899266435,
)


def project(table, shift):
    xpos = table[0] - shift[0]
    ypos = table[1] - shift[1]
    zpos = table[2] - shift[2]
    scales = [jnp.exp(table[3 + k]) for k in range(3)]
    quat = table[6:10]
    norm = 1.0 / jnp.sqrt(sum(part * part for part in quat))
    qw, qx, qy, qz = (part * norm for part in quat)
    rot = [
        [1 - 2 * (qy * qy + qz * qz), 2 * (qx * qy - qw * qz), 2 * (qx * qz + qw * qy)],
        [2 * (qx * qy + qw * qz), 1 - 2 * (qx * qx + qz * qz), 2 * (qy * qz - qw * qx)],
        [2 * (qx * qz - qw * qy), 2 * (qy * qz + qw * qx), 1 - 2 * (qx * qx + qy * qy)],
    ]
    inverse_z = 1.0 / zpos
    mean_u = xpos * inverse_z
    mean_v = ypos * inverse_z
    stretch = [scale * inverse_z for scale in scales]
    first = [(rot[0][k] - mean_u * rot[2][k]) * stretch[k] for k in range(3)]
    second = [(rot[1][k] - mean_v * rot[2][k]) * stretch[k] for k in range(3)]
    cov_a = first[0] * first[0] + first[1] * first[1] + first[2] * first[2] + 8e-08
    cov_b = first[0] * second[0] + first[1] * second[1] + first[2] * second[2]
    cov_c = second[0] * second[0] + second[1] * second[1] + second[2] * second[2] + 8e-08
    over_det = 1.0 / (cov_a * cov_c - cov_b * cov_b)
    over_length = 1.0 / jnp.sqrt(xpos * xpos + ypos * ypos + zpos * zpos)
    dx, dy, dz = (xpos * over_length, ypos * over_length, zpos * over_length)
    xx, yy, zz = (dx * dx, dy * dy, dz * dz)
    basis = [
        -sh_c1 * dy,
        sh_c1 * dz,
        -sh_c1 * dx,
        sh_c2[0] * dx * dy,
        sh_c2[1] * dy * dz,
        sh_c2[2] * (2 * zz - xx - yy),
        sh_c2[3] * dx * dz,
        sh_c2[4] * (xx - yy),
        sh_c3[0] * dy * (3 * xx - yy),
        sh_c3[1] * dx * dy * dz,
        sh_c3[2] * dy * (4 * zz - xx - yy),
        sh_c3[3] * dz * (2 * zz - 3 * xx - 3 * yy),
        sh_c3[4] * dx * (4 * zz - xx - yy),
        sh_c3[5] * dz * (xx - yy),
        sh_c3[6] * dx * (xx - 3 * yy),
    ]
    colors = []
    for k in range(3):
        total = 0.5 + sh_c0 * table[11 + 16 * k]
        for j, part in enumerate(basis):
            total = total + part * table[12 + 16 * k + j]
        colors.append(jnp.maximum(total, 0.0))
    opacity = 1.0 / (1.0 + jnp.exp(-table[10]))
    return [
        mean_u,
        mean_v,
        cov_c * over_det,
        -cov_b * over_det,
        cov_a * over_det,
        opacity,
        colors[0],
        colors[1],
        colors[2],
    ]


def pieces(value, count):
    out = []
    for left in range(count - 1, -1, -1):
        part = value.astype(bf16)
        out.append(part)
        if left:
            value = value - part.astype(f32)
    return out


def dot(one, other):
    return jnp.dot(one, other, preferred_element_type=f32)


def one_hot(low_row):
    rows = lax.broadcasted_iota(i32, (WIDE, WIDE), 0).astype(f32).astype(bf16)
    low = jnp.broadcast_to(low_row.astype(f32).astype(bf16), (WIDE, WIDE))
    return jnp.where(rows == low, jnp.ones((WIDE, WIDE), bf16), jnp.zeros((WIDE, WIDE), bf16))


def get(ref, start, count, stride=1, many=WIDE):
    rows = pl.ds(start, count, stride=stride) if stride > 1 else pl.ds(start, count)
    return jnp.concatenate([ref[h, rows, :] for h in range(many // 128)], axis=1)


def put(ref, start, count, value, stride=1):
    rows = pl.ds(start, count, stride=stride) if stride > 1 else pl.ds(start, count)
    for h in range(value.shape[1] // 128):
        ref[h, rows, :] = value[:, 128 * h : 128 * h + 128]


def invert(index_ref, inverse_ref):
    blocks = index_ref.shape[0]
    high_rows = lax.broadcasted_iota(i32, (blocks, WIDE), 0)
    lanes = lax.broadcasted_iota(i32, (blocks, WIDE), 1).astype(f32)
    wide_lanes = lax.broadcasted_iota(i32, (WIDE, WIDE), 1).astype(f32)
    lows = (index_ref[...] & (WIDE - 1)).astype(f32).T.astype(bf16)
    thin = wide_lanes.astype(bf16)
    ones, zeros = jnp.ones((WIDE, WIDE), bf16), jnp.zeros((WIDE, WIDE), bf16)
    total = None
    for j in range(blocks):
        here = high_rows == lax.shift_right_logical(index_ref[j : j + 1, :], 8)
        left = jnp.concatenate([jnp.where(here, float(j), 0.0), jnp.where(here, lanes, 0.0)], axis=0)
        low = jnp.broadcast_to(lows[:, j : j + 1], (WIDE, WIDE))
        part = dot(left.astype(bf16), jnp.where(thin == low, ones, zeros))
        total = part if total is None else total + part
    found = total[:blocks] * float(WIDE) + total[blocks:]
    inverse_ref[...] = found.astype(i32)


def permute(held_ref, index_ref, count, give):
    blocks = index_ref.shape[0]
    rows = ATTRS * blocks
    stack = jnp.concatenate(pieces(get(held_ref, 0, rows), count), axis=0)
    high_rows = lax.broadcasted_iota(i32, (blocks, WIDE), 0)
    for j in range(blocks):
        row = index_ref[j : j + 1, :]
        spread = one_hot(row & (WIDE - 1))
        high = lax.shift_right_logical(row, 8)
        both = dot(stack, spread)
        found = both[:rows]
        for k in range(1, count):
            found = found + both[k * rows : (k + 1) * rows]
        high_eight = jnp.broadcast_to(high, (8, WIDE))
        eight = found[0:8]
        for b in range(1, blocks):
            eight = jnp.where(high_eight == b, found[8 * b : 8 * b + 8], eight)
        ninth = jnp.sum(jnp.where(high_rows == high, found[8 * blocks :], 0.0), axis=0, keepdims=True)
        give(j, eight, ninth)


def put_travel(out_ref, blocks, packed, j, eight, ninth):
    for h in range(2):
        half = slice(128 * h, 128 * h + 128)
        if packed:
            out_ref[18 * j + 8 * h : 18 * j + 8 * h + 8, :] = eight[:, half]
            out_ref[18 * j + 16 + h : 18 * j + 17 + h, :] = ninth[:, half]
        else:
            out_ref[pl.ds(2 * j + h, 8, stride=2 * blocks), :] = eight[:, half]
            out_ref[16 * blocks + 2 * j + h : 16 * blocks + 2 * j + h + 1, :] = ninth[:, half]


def take_travel(in_ref, held_ref, blocks, packed):
    for j in range(blocks):
        for h in range(2):
            if packed:
                held_ref[h, 8 * j : 8 * j + 8, :] = in_ref[18 * j + 8 * h : 18 * j + 8 * h + 8, :]
                held_ref[h, 8 * blocks + j : 8 * blocks + j + 1, :] = in_ref[18 * j + 16 + h : 18 * j + 17 + h, :]
            else:
                held_ref[h, 8 * j : 8 * j + 8, :] = in_ref[pl.ds(2 * j + h, 8, stride=2 * blocks), :]
                held_ref[h, 8 * blocks + j : 8 * blocks + j + 1, :] = in_ref[
                    16 * blocks + 2 * j + h : 16 * blocks + 2 * j + h + 1, :
                ]


def spread_scalars(values, tiles):
    rows = lax.broadcasted_iota(i32, (tiles, WIDE), 0)
    out = jnp.full((tiles, WIDE), values[0], values[0].dtype)
    for t in range(1, tiles):
        out = jnp.where(rows == t, values[t], out)
    return out


def dense_kernel(params_ref, dense_ref):
    width, count = params_ref.shape
    blocks = count // WIDE
    for first in range(0, width, 8):
        rows = min(8, width - first)
        for j in range(blocks):
            value = params_ref[first : first + rows, WIDE * j : WIDE * (j + 1)]
            put(dense_ref, first * blocks + j, rows, value, blocks)


def prepare_kernel(
    member_ref,
    grad_ref,
    length_ref,
    place_ref,
    cam_ref,
    inverse_ref,
    light_ref,
    turned_ref,
    centre_ref,
    camera_ref,
    plan_ref,
    light,
):
    tiles = grad_ref.shape[1]
    across = [lax.rem(place_ref[t], ACROSS).astype(f32) for t in range(tiles)]
    down = [lax.div(place_ref[t], ACROSS).astype(f32) for t in range(tiles)]
    centre_ref[0] = spread_scalars([(x * SIDE + SIDE / 2) / SCALE - 1.0 for x in across], tiles)
    centre_ref[1] = spread_scalars([(y * SIDE + SIDE / 2) / SCALE - 0.5625 for y in down], tiles)
    lengths = spread_scalars([length_ref[t] for t in range(tiles)], tiles)
    live = lax.broadcasted_iota(i32, (tiles, WIDE), 1) < lengths
    centre_ref[2] = jnp.where(live, 1.0, 0.0)
    views = cam_ref.shape[1]
    for axis in range(3):
        for k in range(views):
            row = axis * views + k
            camera_ref[row : row + 1, :] = jnp.full((1, WIDE), cam_ref[axis, k], f32)
    wide = [(length_ref[t] > WIDE // 2).astype(i32) for t in range(tiles)]
    many = sum(wide[1:], wide[0])
    first, last = jnp.int32(0), many
    for t in range(tiles):
        plan_ref[jnp.where(wide[t] > 0, first, last)] = t
        first, last = first + wide[t], last + 1 - wide[t]
    plan_ref[tiles] = lax.div(many + GROUP - 1, GROUP)

    invert(member_ref, inverse_ref)

    light[...] = jnp.zeros_like(light)
    for t in range(tiles):
        high, low = pieces(jnp.concatenate([grad_ref[k, t : t + 1, :] for k in range(3)], axis=0), 2)
        light[16 * t : 16 * t + 3, :] = high.astype(f32)
        light[16 * t + 3 : 16 * t + 6, :] = low.astype(f32)
        light[16 * t + 6 : 16 * t + 9, :] = high.astype(f32)
    light_ref[...] = light[...].astype(bf16)
    for t in range(tiles):
        turned_ref[t] = light[16 * t : 16 * t + 16, :].T.astype(bf16)


def shifts(inverse, slots_per, camera_ref):
    views = camera_ref.shape[0] // 3
    view = lax.rem(lax.div(inverse, slots_per), views)
    out = []
    for axis in range(3):
        rows = [camera_ref[axis * views + k : axis * views + k + 1, :] for k in range(views)]
        value = jnp.broadcast_to(rows[0], inverse.shape)
        for k in range(1, views):
            value = jnp.where(view == k, rows[k], value)
        out.append(value)
    return out


def dense_rows(ref, count, blocks):
    return [get(ref, k * blocks, blocks) for k in range(count)]


def owner_kernel(slots_per, packed, asked_ref, dense_ref, camera_ref, attrs_ref, inverse_ref, held):
    blocks = asked_ref.shape[0]
    width = dense_ref.shape[1] // blocks
    invert(asked_ref, inverse_ref)
    shift = shifts(inverse_ref[...], slots_per, camera_ref)
    attrs = project(dense_rows(dense_ref, width, blocks), shift)
    for a in range(8):
        put(held, a, blocks, attrs[a], 8)
    put(held, 8 * blocks, blocks, attrs[8])
    permute(held, asked_ref, 3, functools.partial(put_travel, attrs_ref, blocks, packed))


def return_kernel(slots_per, packed, back_ref, inverse_ref, dense_ref, camera_ref, out_ref, held, flat, grads):
    blocks = inverse_ref.shape[0]
    width = dense_ref.shape[1] // blocks
    take_travel(back_ref, held, blocks, packed)

    def give(j, eight, ninth):
        put(flat, j, 8, eight, blocks)
        put(flat, 8 * blocks + j, 1, ninth)

    permute(held, inverse_ref, 2, give)
    shift = shifts(inverse_ref[...], slots_per, camera_ref)
    _, back = jax.vjp(lambda rows: project(rows, shift), dense_rows(dense_ref, width, blocks))
    (rows,) = back(dense_rows(flat, ATTRS, blocks))
    for k in range(width):
        put(grads, k * blocks, blocks, rows[k])
    for first in range(0, width, 8):
        count = min(8, width - first)
        for j in range(blocks):
            value = get(grads, first * blocks + j, count, blocks)
            out_ref[first : first + count, WIDE * j : WIDE * (j + 1)] = value


def offsets(index):
    column = lax.rem(index, SIDE).astype(f32) - (SIDE - 1) / 2
    row = lax.div(index, SIDE).astype(f32) - (SIDE - 1) / 2
    return column, row


def pick(index, choices):
    out = jnp.zeros(index.shape, f32)
    for k, choice in enumerate(choices):
        out = jnp.where(index == k, choice, out)
    return out


def render_kernel(
    packed,
    arrived_ref,
    member_ref,
    inverse_ref,
    light_ref,
    turned_ref,
    centre_ref,
    plan_ref,
    image_ref,
    back_ref,
    image,
    sent,
    held,
    flat,
    coefs,
    sums,
    upper,
    lower,
    monomials,
    moments,
):
    tiles = member_ref.shape[0]
    blocks = tiles
    take_travel(arrived_ref, held, blocks, packed)

    def give(j, eight, ninth):
        put(flat, j, 8, eight, blocks)
        put(flat, 8 * blocks + j, 1, ninth)

    permute(held, member_ref, 3, give)

    mu, nu, con_a, con_b, con_c, opacity, *colors = dense_rows(flat, ATTRS, blocks)
    centre_u, centre_v, live = (centre_ref[k] for k in range(3))
    live = live > 0.0
    m = (mu - centre_u) * SCALE
    n = (nu - centre_v) * SCALE
    unit = LOG2E / (SCALE * SCALE)
    a = con_a * (-0.5 * unit)
    b = con_b * -unit
    c = con_c * (-0.5 * unit)
    lift = -2.0 * a * m - b * n
    tilt = -2.0 * c * n - b * m
    rest = -0.5 * (lift * m + tilt * n) + jnp.log2(opacity)
    terms = [a, b, c, lift, tilt]
    terms = [jnp.where(live, term, 0.0) for term in terms] + [jnp.where(live, rest, FAR)]
    coefs[...] = jnp.zeros_like(coefs)
    for k, term in enumerate(terms):
        for s, part in enumerate(pieces(term, 3)):
            row = 6 * s + k
            put(coefs, row * tiles, tiles, part.astype(f32))
    for k, color in enumerate(colors):
        high, low = (part.astype(f32) for part in pieces(color, 2))
        for row, part in ((32 + k, high), (35 + k, high), (38 + k, low)):
            put(coefs, row * tiles, tiles, part)

    row_index = lax.broadcasted_iota(i32, (WIDE, WIDE), 0)
    lane_index = lax.broadcasted_iota(i32, (WIDE, WIDE), 1)
    upper[...] = jnp.where(row_index < lane_index, 1.0, 0.0).astype(bf16)
    lower[...] = jnp.where(row_index > lane_index, 1.0, 0.0).astype(bf16)
    column, row = offsets(lax.broadcasted_iota(i32, (WIDE, 32), 0))
    which = lax.broadcasted_iota(i32, (WIDE, 32), 1)
    which = jnp.where(which < 18, lax.rem(which, 6), 6)
    one = jnp.ones((WIDE, 32), f32)
    monomials[...] = pick(
        which, [column * column, column * row, row * row, column, row, one]
    ).astype(bf16)
    column, row = offsets(lax.broadcasted_iota(i32, (16, WIDE), 1))
    which = lax.broadcasted_iota(i32, (16, WIDE), 0)
    one = jnp.ones((16, WIDE), f32)
    moments[...] = pick(
        which, [column * column, column * row, row * row, column, row, one]
    ).astype(bf16)
    sums[...] = jnp.zeros_like(sums)

    def some_tiles(turn, many):
        ts = [plan_ref[GROUP * turn + k] for k in range(GROUP)]
        block = [pl.ds(pl.multiple_of(16 * t, 16), 16) for t in ts]
        coef = [get(coefs, t, 32, tiles, many).astype(bf16) for t in ts]
        color = [get(coefs, t + 32 * tiles, 16, tiles, many).astype(bf16) for t in ts]
        power = [jnp.exp2(dot(monomials[...], x)) for x in coef]
        alpha = [jnp.minimum(x, 0.99) for x in power]
        keep = [1.0 - x for x in alpha]
        parts = [pieces(jnp.log2(x), 2) for x in keep]
        before = upper[:many, :many]
        through = [jnp.exp2(dot(high, before) + dot(low, before)) for high, low in parts]
        pull = [dot(turned_ref[t], x) for t, x in zip(ts, color)]
        weight = [x * y for x, y in zip(alpha, through)]
        parts = [pieces(x * y, 2) for x, y in zip(pull, weight)]
        after = lower[:many, :many]
        behind = [dot(high, after) + dot(low, after) for high, low in parts]
        parts = [pieces(x, 2) for x in weight]
        for t, x, (high, low) in zip(ts, color, parts):
            turned = x.astype(f32).T.astype(bf16)
            picture = (dot(high, turned) + dot(low, turned)).T
            for channel in range(3):
                image[channel, pl.ds(t, 1), :] = picture[channel : channel + 1] + picture[channel + 6 : channel + 7]
        for t, rows, (high, low) in zip(ts, block, parts):
            tint = dot(light_ref[rows, :], high) + dot(light_ref[rows, :], low)
            put(sums, pl.multiple_of(16 * t + 8, 8), 8, tint[0:8] + pltpu.roll(tint[0:8], 5, 0))
        for k, t in enumerate(ts):
            slope = (pull[k] * through[k] - behind[k] / keep[k]) * alpha[k]
            high, low = pieces(jnp.where(power[k] < 0.99, slope, 0.0), 2)
            moment = dot(moments[...], high) + dot(moments[...], low)
            put(sums, pl.multiple_of(16 * t, 16), 8, moment[0:8])

    def wide_turn(turn, carry):
        some_tiles(turn, WIDE)
        return carry

    def narrow_turn(turn, carry):
        some_tiles(turn, WIDE // 2)
        return carry

    wide_turns = plan_ref[tiles]
    lax.fori_loop(0, wide_turns, wide_turn, 0)
    lax.fori_loop(wide_turns, tiles // GROUP, narrow_turn, 0)
    send = pltpu.make_async_copy(image, image_ref, sent)
    send.start()

    m_xx, m_xy, m_yy, m_x, m_y, m_one = [get(sums, k, tiles, 16) for k in range(6)]
    d_x = m_x - m * m_one
    d_y = m_y - n * m_one
    d_xx = m_xx - m * (m_x + d_x)
    d_xy = m_xy - m * m_y - n * d_x
    d_yy = m_yy - n * (m_y + d_y)
    shrink = 1.0 / SCALE
    grads = [
        (con_a * d_x + con_b * d_y) * shrink,
        (con_c * d_y + con_b * d_x) * shrink,
        d_xx * (-0.5 * shrink * shrink),
        d_xy * (-shrink * shrink),
        d_yy * (-0.5 * shrink * shrink),
        m_one / opacity,
        *[get(sums, 8 + k, tiles, 16) for k in range(3)],
    ]
    for k in range(8):
        put(held, k, blocks, grads[k], 8)
    put(held, 8 * blocks, blocks, grads[8])
    permute(held, inverse_ref, 2, functools.partial(put_travel, back_ref, blocks, packed))
    send.wait()


def vmem(count):
    return [pl.BlockSpec(memory_space=pltpu.VMEM)] * count


def far(count):
    return [pl.BlockSpec(memory_space=pltpu.HBM)] * count


def smem(count):
    return [pl.BlockSpec(memory_space=pltpu.SMEM)] * count


def shape(*dims, dtype=f32):
    return jax.ShapeDtypeStruct(dims, dtype)


def call(kernel, name, ins, outs, scratch, cycles, places=None):
    return pl.pallas_call(
        kernel,
        out_shape=outs,
        in_specs=ins,
        out_specs=places or vmem(len(outs)),
        scratch_shapes=scratch,
        name=name,
        compiler_params=pltpu.CompilerParams(vmem_limit_bytes=48 * 1024 * 1024),
        cost_estimate=pl.CostEstimate(flops=cycles, bytes_accessed=4_000_000, transcendentals=0),
    )


def travel(rows, peers, slots, packed):
    total = rows.shape[0]
    if packed:
        parts = rows.reshape(peers, 1, -1)
    else:
        parts = jnp.swapaxes(rows.reshape(ATTRS, peers, slots), 0, 1)
    parts = lax.all_to_all(parts, "gs", split_axis=0, concat_axis=0, tiled=True)
    if not packed:
        parts = jnp.swapaxes(parts, 0, 1)
    return parts.reshape(total, 128)


def on_device(params, requests, member, tile_len, tile_pos, cam_shift, pixel_grad):
    peers, slots = requests.shape
    width, count = params.shape
    tiles = member.shape[0]
    blocks = count // WIDE
    packed = slots % WIDE == 0
    held = pltpu.VMEM((2, ATTRS * blocks, 128), f32)
    rows = shape(18 * blocks, 128)
    index = shape(blocks, WIDE, dtype=i32)

    asked = lax.all_to_all(requests, "gs", split_axis=0, concat_axis=0, tiled=True)
    asked = asked.reshape(blocks, WIDE)
    (dense,) = call(dense_kernel, "dense", vmem(1), [shape(2, width * blocks, 128)], [], 1_000_000)(params)
    inverse, light, turned, centre, camera, plan = call(
        prepare_kernel,
        "prepare",
        vmem(2) + smem(3),
        [
            index,
            shape(16 * tiles, WIDE, dtype=bf16),
            shape(tiles, WIDE, 16, dtype=bf16),
            shape(3, tiles, WIDE),
            shape(3 * cam_shift.shape[1], WIDE),
            shape(tiles + 1, dtype=i32),
        ],
        [
            pltpu.VMEM((16 * tiles, WIDE), f32),
        ],
        10_000_000,
        vmem(5) + smem(1),
    )(member, jnp.swapaxes(pixel_grad, 0, 1), tile_len, tile_pos, cam_shift)
    attrs, place = call(
        functools.partial(owner_kernel, slots, packed),
        "owner",
        vmem(3),
        [rows, index],
        [held],
        10_000_000,
    )(asked, dense, camera)
    arrived = travel(attrs, peers, slots, packed)
    image, back = call(
        functools.partial(render_kernel, packed),
        "render",
        vmem(6) + smem(1),
        [shape(3, tiles, WIDE), rows],
        [
            pltpu.VMEM((3, tiles, WIDE), f32),
            pltpu.SemaphoreType.DMA,
            held,
            held,
            pltpu.VMEM((2, 48 * tiles, 128), f32),
            pltpu.VMEM((2, 16 * tiles, 128), f32),
            pltpu.VMEM((WIDE, WIDE), bf16),
            pltpu.VMEM((WIDE, WIDE), bf16),
            pltpu.VMEM((WIDE, 32), bf16),
            pltpu.VMEM((16, WIDE), bf16),
        ],
        100_000_000,
        far(1) + vmem(1),
    )(arrived, member, inverse, light, turned, centre, plan)
    returned = travel(back, peers, slots, packed)
    (grad_params,) = call(
        functools.partial(return_kernel, slots, packed),
        "return",
        vmem(4),
        [shape(width, count)],
        [held, held, pltpu.VMEM((2, width * blocks, 128), f32)],
        10_000_000,
    )(returned, place, dense, camera)
    return (jnp.swapaxes(image, 0, 1), grad_params)


def solution(mesh):
    return jax.shard_map(
        on_device,
        mesh=mesh,
        in_specs=(
            P(None, ("groups", "gs")),
            P(("groups", "gs"), None),
            P(("groups", "gs"), None),
            P(("groups", "gs")),
            P(("groups", "gs")),
            P(None, "groups"),
            P(("groups", "gs"), None, None),
        ),
        out_specs=(P(("groups", "gs"), None, None), P(None, ("groups", "gs"))),
        check_vma=False,
    )
```

```python
import functools

import jax
import jax.numpy as jnp
from jax import lax
from jax.experimental import pallas as pl
from jax.experimental.pallas import tpu as pltpu
from jax.sharding import PartitionSpec as P

f32, bf16, i32 = jnp.float32, jnp.bfloat16, jnp.int32

WIDE = 256
ATTRS = 9
SIDE = 16
ACROSS = 240
SCALE = 1920.0
LOG2E = 1.4426950408889634
GROUP = 4
FAR = -1.0e9

sh_c0 = 0.28209479177387814
sh_c1 = 0.4886025119029199
sh_c2 = (
    1.0925484305920792,
    -1.0925484305920792,
    0.31539156525252005,
    -1.0925484305920792,
    0.5462742152960396,
)
sh_c3 = (
    -0.5900435899266435,
    2.890611442640554,
    -0.4570457994644658,
    0.3731763325901154,
    -0.4570457994644658,
    1.445305721320277,
    -0.5900435899266435,
)


def outline(table, shift):
    xpos = table[0] - shift[0]
    ypos = table[1] - shift[1]
    zpos = table[2] - shift[2]
    scales = [jnp.exp(table[3 + k]) for k in range(3)]
    quat = table[6:10]
    norm = 1.0 / jnp.sqrt(sum(part * part for part in quat))
    qw, qx, qy, qz = (part * norm for part in quat)
    rot = [
        [1 - 2 * (qy * qy + qz * qz), 2 * (qx * qy - qw * qz), 2 * (qx * qz + qw * qy)],
        [2 * (qx * qy + qw * qz), 1 - 2 * (qx * qx + qz * qz), 2 * (qy * qz - qw * qx)],
        [2 * (qx * qz - qw * qy), 2 * (qy * qz + qw * qx), 1 - 2 * (qx * qx + qy * qy)],
    ]
    inverse_z = 1.0 / zpos
    mean_u = xpos * inverse_z
    mean_v = ypos * inverse_z
    stretch = [scale * inverse_z for scale in scales]
    first = [(rot[0][k] - mean_u * rot[2][k]) * stretch[k] for k in range(3)]
    second = [(rot[1][k] - mean_v * rot[2][k]) * stretch[k] for k in range(3)]
    cov_a = first[0] * first[0] + first[1] * first[1] + first[2] * first[2] + 8e-08
    cov_b = first[0] * second[0] + first[1] * second[1] + first[2] * second[2]
    cov_c = second[0] * second[0] + second[1] * second[1] + second[2] * second[2] + 8e-08
    over_det = 1.0 / (cov_a * cov_c - cov_b * cov_b)
    opacity = 1.0 / (1.0 + jnp.exp(-table[10]))
    return [mean_u, mean_v, cov_c * over_det, -cov_b * over_det, cov_a * over_det, opacity]


def tints(place, coefs, shift):
    xpos = place[0] - shift[0]
    ypos = place[1] - shift[1]
    zpos = place[2] - shift[2]
    over_length = 1.0 / jnp.sqrt(xpos * xpos + ypos * ypos + zpos * zpos)
    dx, dy, dz = (xpos * over_length, ypos * over_length, zpos * over_length)
    xx, yy, zz = (dx * dx, dy * dy, dz * dz)
    basis = [
        -sh_c1 * dy,
        sh_c1 * dz,
        -sh_c1 * dx,
        sh_c2[0] * dx * dy,
        sh_c2[1] * dy * dz,
        sh_c2[2] * (2 * zz - xx - yy),
        sh_c2[3] * dx * dz,
        sh_c2[4] * (xx - yy),
        sh_c3[0] * dy * (3 * xx - yy),
        sh_c3[1] * dx * dy * dz,
        sh_c3[2] * dy * (4 * zz - xx - yy),
        sh_c3[3] * dz * (2 * zz - 3 * xx - 3 * yy),
        sh_c3[4] * dx * (4 * zz - xx - yy),
        sh_c3[5] * dz * (xx - yy),
        sh_c3[6] * dx * (xx - 3 * yy),
    ]
    colors = []
    for k in range(3):
        total = 0.5 + sh_c0 * coefs[16 * k]
        for j, part in enumerate(basis):
            total = total + part * coefs[16 * k + 1 + j]
        colors.append(jnp.maximum(total, 0.0))
    return colors


def pieces(value, count):
    out = []
    for left in range(count - 1, -1, -1):
        part = value.astype(bf16)
        out.append(part)
        if left:
            value = value - part.astype(f32)
    return out


def dot(one, other):
    return jnp.dot(one, other, preferred_element_type=f32)


def stacked(high, low, weights):
    rows = high.shape[0]
    both = dot(jnp.concatenate([high, low], axis=0), weights)
    return both[:rows] + both[rows:]


def one_hot(low_row):
    rows = lax.broadcasted_iota(i32, (WIDE, WIDE), 0).astype(f32).astype(bf16)
    low = jnp.broadcast_to(low_row.astype(f32).astype(bf16), (WIDE, WIDE))
    return jnp.where(rows == low, jnp.ones((WIDE, WIDE), bf16), jnp.zeros((WIDE, WIDE), bf16))


def get(ref, start, count, stride=1, many=WIDE):
    rows = pl.ds(start, count, stride=stride) if stride > 1 else pl.ds(start, count)
    return jnp.concatenate([ref[h, rows, :] for h in range(many // 128)], axis=1)


def put(ref, start, count, value, stride=1):
    rows = pl.ds(start, count, stride=stride) if stride > 1 else pl.ds(start, count)
    for h in range(value.shape[1] // 128):
        ref[h, rows, :] = value[:, 128 * h : 128 * h + 128]


def invert(index_ref, inverse_ref):
    blocks = index_ref.shape[0]
    high_rows = lax.broadcasted_iota(i32, (blocks, WIDE), 0)
    lanes = lax.broadcasted_iota(i32, (blocks, WIDE), 1).astype(f32)
    wide_lanes = lax.broadcasted_iota(i32, (WIDE, WIDE), 1).astype(f32)
    lows = (index_ref[...] & (WIDE - 1)).astype(f32).T.astype(bf16)
    thin = wide_lanes.astype(bf16)
    ones, zeros = jnp.ones((WIDE, WIDE), bf16), jnp.zeros((WIDE, WIDE), bf16)
    total = None
    for j in range(blocks):
        here = high_rows == lax.shift_right_logical(index_ref[j : j + 1, :], 8)
        left = jnp.concatenate([jnp.where(here, float(j), 0.0), jnp.where(here, lanes, 0.0)], axis=0)
        low = jnp.broadcast_to(lows[:, j : j + 1], (WIDE, WIDE))
        part = dot(left.astype(bf16), jnp.where(thin == low, ones, zeros))
        total = part if total is None else total + part
    found = total[:blocks] * float(WIDE) + total[blocks:]
    inverse_ref[...] = found.astype(i32)


def permute(held_ref, index_ref, fine, give):
    blocks = index_ref.shape[0]
    rows = ATTRS * blocks
    thirds = [pieces(get(held_ref, a, blocks, 8), 3)[2] for a in range(fine)]
    stack = jnp.concatenate(pieces(get(held_ref, 0, rows), 2) + thirds, axis=0)
    high_rows = lax.broadcasted_iota(i32, (blocks, WIDE), 0)
    place = lax.broadcasted_iota(i32, (8, WIDE), 0)
    for j in range(blocks):
        row = index_ref[j : j + 1, :]
        high = lax.shift_right_logical(row, 8)
        here = high_rows == high
        both = dot(stack, one_hot(row & (WIDE - 1)))
        found = both[:rows] + both[rows : 2 * rows]
        high_eight = jnp.broadcast_to(high, (8, WIDE))
        eight = found[0:8]
        for b in range(1, blocks):
            eight = jnp.where(high_eight == b, found[8 * b : 8 * b + 8], eight)

        def single(values):
            return jnp.sum(jnp.where(here, values, 0.0), axis=0, keepdims=True)

        for a in range(fine):
            start = 2 * rows + a * blocks
            eight = eight + jnp.where(place == a, single(both[start : start + blocks]), 0.0)
        give(j, eight, single(found[8 * blocks :]))


def put_travel(out_ref, blocks, packed, j, eight, ninth):
    for h in range(2):
        half = slice(128 * h, 128 * h + 128)
        if packed:
            out_ref[18 * j + 8 * h : 18 * j + 8 * h + 8, :] = eight[:, half]
            out_ref[18 * j + 16 + h : 18 * j + 17 + h, :] = ninth[:, half]
        else:
            out_ref[pl.ds(2 * j + h, 8, stride=2 * blocks), :] = eight[:, half]
            out_ref[16 * blocks + 2 * j + h : 16 * blocks + 2 * j + h + 1, :] = ninth[:, half]


def take_travel(in_ref, held_ref, blocks, packed):
    for j in range(blocks):
        for h in range(2):
            if packed:
                held_ref[h, 8 * j : 8 * j + 8, :] = in_ref[18 * j + 8 * h : 18 * j + 8 * h + 8, :]
                held_ref[h, 8 * blocks + j : 8 * blocks + j + 1, :] = in_ref[18 * j + 16 + h : 18 * j + 17 + h, :]
            else:
                held_ref[h, 8 * j : 8 * j + 8, :] = in_ref[pl.ds(2 * j + h, 8, stride=2 * blocks), :]
                held_ref[h, 8 * blocks + j : 8 * blocks + j + 1, :] = in_ref[
                    16 * blocks + 2 * j + h : 16 * blocks + 2 * j + h + 1, :
                ]


def spread_scalars(values, tiles):
    rows = lax.broadcasted_iota(i32, (tiles, WIDE), 0)
    out = jnp.full((tiles, WIDE), values[0], values[0].dtype)
    for t in range(1, tiles):
        out = jnp.where(rows == t, values[t], out)
    return out


def dense_kernel(params_ref, dense_ref):
    width, count = params_ref.shape
    blocks = count // WIDE
    for first in range(0, width, 8):
        rows = min(8, width - first)
        for j in range(blocks):
            value = params_ref[first : first + rows, WIDE * j : WIDE * (j + 1)]
            put(dense_ref, first * blocks + j, rows, value, blocks)


def prepare_kernel(
    member_ref,
    grad_ref,
    length_ref,
    place_ref,
    cam_ref,
    inverse_ref,
    light_ref,
    turned_ref,
    centre_ref,
    camera_ref,
    plan_ref,
    light,
):
    tiles = grad_ref.shape[1]
    across = [lax.rem(place_ref[t], ACROSS).astype(f32) for t in range(tiles)]
    down = [lax.div(place_ref[t], ACROSS).astype(f32) for t in range(tiles)]
    centre_ref[0] = spread_scalars([(x * SIDE + SIDE / 2) / SCALE - 1.0 for x in across], tiles)
    centre_ref[1] = spread_scalars([(y * SIDE + SIDE / 2) / SCALE - 0.5625 for y in down], tiles)
    lengths = spread_scalars([length_ref[t] for t in range(tiles)], tiles)
    live = lax.broadcasted_iota(i32, (tiles, WIDE), 1) < lengths
    centre_ref[2] = jnp.where(live, 1.0, 0.0)
    views = cam_ref.shape[1]
    for axis in range(3):
        for k in range(views):
            row = axis * views + k
            camera_ref[row : row + 1, :] = jnp.full((1, WIDE), cam_ref[axis, k], f32)
    wide = [(length_ref[t] > WIDE // 2).astype(i32) for t in range(tiles)]
    many = sum(wide[1:], wide[0])
    first, last = jnp.int32(0), many
    for t in range(tiles):
        plan_ref[jnp.where(wide[t] > 0, first, last)] = t
        first, last = first + wide[t], last + 1 - wide[t]
    plan_ref[tiles] = lax.div(many + GROUP - 1, GROUP)

    invert(member_ref, inverse_ref)

    light[...] = jnp.zeros_like(light)
    for t in range(tiles):
        high, low = pieces(jnp.concatenate([grad_ref[k, t : t + 1, :] for k in range(3)], axis=0), 2)
        light[16 * t : 16 * t + 3, :] = high.astype(f32)
        light[16 * t + 3 : 16 * t + 6, :] = low.astype(f32)
        light[16 * t + 6 : 16 * t + 9, :] = high.astype(f32)
    light_ref[...] = light[...].astype(bf16)
    for t in range(tiles):
        turned_ref[t] = light[16 * t : 16 * t + 16, :].T.astype(bf16)


def shifts(inverse, slots_per, camera_ref):
    views = camera_ref.shape[0] // 3
    view = lax.rem(lax.div(inverse, slots_per), views)
    out = []
    for axis in range(3):
        rows = [camera_ref[axis * views + k : axis * views + k + 1, :] for k in range(views)]
        value = jnp.broadcast_to(rows[0], inverse.shape)
        for k in range(1, views):
            value = jnp.where(view == k, rows[k], value)
        out.append(value)
    return out


def dense_rows(ref, count, blocks):
    return [get(ref, k * blocks, blocks) for k in range(count)]


def owner_kernel(slots_per, packed, asked_ref, dense_ref, camera_ref, attrs_ref, inverse_ref, held):
    blocks = asked_ref.shape[0]
    width = dense_ref.shape[1] // blocks
    invert(asked_ref, inverse_ref)
    shift = shifts(inverse_ref[...], slots_per, camera_ref)
    table = dense_rows(dense_ref, width, blocks)
    attrs = outline(table, shift) + tints(table[:3], table[11:], shift)
    for a in range(8):
        put(held, a, blocks, attrs[a], 8)
    put(held, 8 * blocks, blocks, attrs[8])
    permute(held, asked_ref, 2, functools.partial(put_travel, attrs_ref, blocks, packed))


def return_kernel(slots_per, packed, back_ref, inverse_ref, dense_ref, camera_ref, out_far, held, flat, grads, out_ref, sent):
    blocks = inverse_ref.shape[0]
    width = dense_ref.shape[1] // blocks
    half = blocks // 2
    take_travel(back_ref, held, blocks, packed)

    sends = []

    def send_rows(first, near):
        count = min(8, width - first)
        for j in range(near, near + half):
            value = get(grads, first * blocks + j, count, blocks)
            out_ref[first : first + count, WIDE * j : WIDE * (j + 1)] = value
        part = (pl.ds(first, count), pl.ds(WIDE * near, WIDE * half))
        sends.append(pltpu.make_async_copy(out_ref.at[part], out_far.at[part], sent.at[len(sends)]))
        sends[-1].start()

    def finish(near):
        table = [get(dense_ref, k * blocks + near, half) for k in range(width)]
        given = [get(flat, k * blocks + near, half) for k in range(ATTRS)]
        shift = shifts(inverse_ref[near : near + half, :], slots_per, camera_ref)
        _, back = jax.vjp(lambda place, coefs: tints(place, coefs, shift), table[:3], table[11:])
        drift, slopes = back(given[6:])
        for k in range(11, width):
            put(grads, k * blocks + near, half, slopes[k - 11])
        for first in range(16, width, 8):
            send_rows(first, near)
        _, back = jax.vjp(lambda rows: outline(rows, shift), table[:11])
        (slopes,) = back(given[:6])
        for k in range(11):
            put(grads, k * blocks + near, half, slopes[k] + drift[k] if k < 3 else slopes[k])
        for first in range(0, 16, 8):
            send_rows(first, near)

    def give(j, eight, ninth):
        put(flat, j, 8, eight, blocks)
        put(flat, 8 * blocks + j, 1, ninth)
        if (j + 1) % half == 0:
            finish(j + 1 - half)

    permute(held, inverse_ref, 0, give)
    for send in sends:
        send.wait()


def offsets(index):
    column = lax.rem(index, SIDE).astype(f32) - (SIDE - 1) / 2
    row = lax.div(index, SIDE).astype(f32) - (SIDE - 1) / 2
    return column, row


def pick(index, choices):
    out = jnp.zeros(index.shape, f32)
    for k, choice in enumerate(choices):
        out = jnp.where(index == k, choice, out)
    return out


def render_kernel(
    packed,
    arrived_ref,
    member_ref,
    inverse_ref,
    light_ref,
    turned_ref,
    centre_ref,
    plan_ref,
    image_ref,
    back_ref,
    image,
    sent,
    held,
    flat,
    coefs,
    sums,
    upper,
    lower,
    monomials,
    moments,
):
    tiles = member_ref.shape[0]
    blocks = tiles
    take_travel(arrived_ref, held, blocks, packed)

    def give(j, eight, ninth):
        put(flat, j, 8, eight, blocks)
        put(flat, 8 * blocks + j, 1, ninth)

    permute(held, member_ref, 2, give)

    mu, nu, con_a, con_b, con_c, opacity, *colors = dense_rows(flat, ATTRS, blocks)
    centre_u, centre_v, live = (centre_ref[k] for k in range(3))
    live = live > 0.0
    m = (mu - centre_u) * SCALE
    n = (nu - centre_v) * SCALE
    unit = LOG2E / (SCALE * SCALE)
    a = con_a * (-0.5 * unit)
    b = con_b * -unit
    c = con_c * (-0.5 * unit)
    lift = -2.0 * a * m - b * n
    tilt = -2.0 * c * n - b * m
    rest = -0.5 * (lift * m + tilt * n) + jnp.log2(opacity)
    terms = [a, b, c, lift, tilt]
    terms = [jnp.where(live, term, 0.0) for term in terms] + [jnp.where(live, rest, FAR)]
    coefs[...] = jnp.zeros_like(coefs)
    for k, term in enumerate(terms):
        for s, part in enumerate(pieces(term, 3)):
            row = 6 * s + k
            put(coefs, row * tiles, tiles, part.astype(f32))
    for k, color in enumerate(colors):
        high, low = (part.astype(f32) for part in pieces(color, 2))
        for row, part in ((32 + k, high), (35 + k, high), (38 + k, low)):
            put(coefs, row * tiles, tiles, part)

    row_index = lax.broadcasted_iota(i32, (WIDE, WIDE), 0)
    lane_index = lax.broadcasted_iota(i32, (WIDE, WIDE), 1)
    upper[...] = jnp.where(row_index < lane_index, 1.0, 0.0).astype(bf16)
    lower[...] = jnp.where(row_index > lane_index, 1.0, 0.0).astype(bf16)
    column, row = offsets(lax.broadcasted_iota(i32, (WIDE, 32), 0))
    which = lax.broadcasted_iota(i32, (WIDE, 32), 1)
    which = jnp.where(which < 18, lax.rem(which, 6), 6)
    one = jnp.ones((WIDE, 32), f32)
    monomials[...] = pick(
        which, [column * column, column * row, row * row, column, row, one]
    ).astype(bf16)
    column, row = offsets(lax.broadcasted_iota(i32, (16, WIDE), 1))
    which = lax.broadcasted_iota(i32, (16, WIDE), 0)
    one = jnp.ones((16, WIDE), f32)
    moments[...] = pick(
        which, [column * column, column * row, row * row, column, row, one]
    ).astype(bf16)
    sums[...] = jnp.zeros_like(sums)

    def some_tiles(turn, many):
        ts = [plan_ref[GROUP * turn + k] for k in range(GROUP)]
        block = [pl.ds(pl.multiple_of(16 * t, 16), 16) for t in ts]
        coef = [get(coefs, t, 32, tiles, many).astype(bf16) for t in ts]
        color = [get(coefs, t + 32 * tiles, 16, tiles, many).astype(bf16) for t in ts]
        alpha = [jnp.minimum(jnp.exp2(dot(monomials[...], x)), 0.99) for x in coef]
        parts = [pieces(jnp.log2(1.0 - x), 2) for x in alpha]
        before = upper[:many, :many]
        through = [jnp.exp2(stacked(high, low, before)) for high, low in parts]
        weight = [x * y for x, y in zip(alpha, through)]
        parts = [pieces(x, 2) for x in weight]
        for t, x, (high, low) in zip(ts, color, parts):
            turned = x.astype(f32).T.astype(bf16)
            picture = stacked(high, low, turned).T
            for channel in range(3):
                image[channel, pl.ds(t, 1), :] = picture[channel : channel + 1] + picture[channel + 6 : channel + 7]
            rows = pl.ds(pl.multiple_of(16 * t, 16), 16)
            lit = light_ref[rows, :]
            tint = dot(jnp.concatenate([lit, lit], axis=1), jnp.concatenate([high, low], axis=0))
            put(sums, pl.multiple_of(16 * t + 8, 8), 8, tint[0:8] + pltpu.roll(tint[0:8], 5, 0))
        pulled = [dot(turned_ref[t], x) * y for t, x, y in zip(ts, color, weight)]
        parts = [pieces(x, 2) for x in pulled]
        after = lower[:many, :many]
        behind = [stacked(high, low, after) for high, low in parts]
        for k, t in enumerate(ts):
            slope = pulled[k] - behind[k] * (alpha[k] / (1.0 - alpha[k]))
            high, low = pieces(jnp.where(alpha[k] < 0.99, slope, 0.0), 2)
            moment = dot(jnp.concatenate([moments[...]] * 2, axis=1), jnp.concatenate([high, low], axis=0))
            put(sums, pl.multiple_of(16 * t, 16), 8, moment[0:8])

    def wide_turn(turn, carry):
        some_tiles(turn, WIDE)
        return carry

    def narrow_turn(turn, carry):
        some_tiles(turn, WIDE // 2)
        return carry

    wide_turns = plan_ref[tiles]
    lax.fori_loop(0, wide_turns, wide_turn, 0)
    lax.fori_loop(wide_turns, tiles // GROUP, narrow_turn, 0)
    send = pltpu.make_async_copy(image, image_ref, sent)
    send.start()

    m_xx, m_xy, m_yy, m_x, m_y, m_one = [get(sums, k, tiles, 16) for k in range(6)]
    d_x = m_x - m * m_one
    d_y = m_y - n * m_one
    d_xx = m_xx - m * (m_x + d_x)
    d_xy = m_xy - m * m_y - n * d_x
    d_yy = m_yy - n * (m_y + d_y)
    shrink = 1.0 / SCALE
    grads = [
        (con_a * d_x + con_b * d_y) * shrink,
        (con_c * d_y + con_b * d_x) * shrink,
        d_xx * (-0.5 * shrink * shrink),
        d_xy * (-shrink * shrink),
        d_yy * (-0.5 * shrink * shrink),
        m_one / opacity,
        *[get(sums, 8 + k, tiles, 16) for k in range(3)],
    ]
    for k in range(8):
        put(held, k, blocks, grads[k], 8)
    put(held, 8 * blocks, blocks, grads[8])
    permute(held, inverse_ref, 0, functools.partial(put_travel, back_ref, blocks, packed))
    send.wait()


def vmem(count):
    return [pl.BlockSpec(memory_space=pltpu.VMEM)] * count


def far(count):
    return [pl.BlockSpec(memory_space=pltpu.HBM)] * count


def smem(count):
    return [pl.BlockSpec(memory_space=pltpu.SMEM)] * count


def shape(*dims, dtype=f32):
    return jax.ShapeDtypeStruct(dims, dtype)


def call(kernel, name, ins, outs, scratch, cycles, places=None):
    return pl.pallas_call(
        kernel,
        out_shape=outs,
        in_specs=ins,
        out_specs=places or vmem(len(outs)),
        scratch_shapes=scratch,
        name=name,
        compiler_params=pltpu.CompilerParams(vmem_limit_bytes=48 * 1024 * 1024),
        cost_estimate=pl.CostEstimate(flops=cycles, bytes_accessed=4_000_000, transcendentals=0),
    )


def travel(rows, peers, slots, packed):
    total = rows.shape[0]
    if packed:
        parts = rows.reshape(peers, 1, -1)
    else:
        parts = jnp.swapaxes(rows.reshape(ATTRS, peers, slots), 0, 1)
    parts = lax.all_to_all(parts, "gs", split_axis=0, concat_axis=0, tiled=True)
    if not packed:
        parts = jnp.swapaxes(parts, 0, 1)
    return parts.reshape(total, 128)


def on_device(params, requests, member, tile_len, tile_pos, cam_shift, pixel_grad):
    peers, slots = requests.shape
    width, count = params.shape
    tiles = member.shape[0]
    blocks = count // WIDE
    packed = slots % WIDE == 0
    held = pltpu.VMEM((2, ATTRS * blocks, 128), f32)
    rows = shape(18 * blocks, 128)
    index = shape(blocks, WIDE, dtype=i32)

    asked = lax.all_to_all(requests, "gs", split_axis=0, concat_axis=0, tiled=True)
    asked = asked.reshape(blocks, WIDE)
    (dense,) = call(dense_kernel, "dense", vmem(1), [shape(2, width * blocks, 128)], [], 1_000_000)(params)
    inverse, light, turned, centre, camera, plan = call(
        prepare_kernel,
        "prepare",
        vmem(2) + smem(3),
        [
            index,
            shape(16 * tiles, WIDE, dtype=bf16),
            shape(tiles, WIDE, 16, dtype=bf16),
            shape(3, tiles, WIDE),
            shape(3 * cam_shift.shape[1], WIDE),
            shape(tiles + 1, dtype=i32),
        ],
        [
            pltpu.VMEM((16 * tiles, WIDE), f32),
        ],
        10_000_000,
        vmem(5) + smem(1),
    )(member, jnp.swapaxes(pixel_grad, 0, 1), tile_len, tile_pos, cam_shift)
    attrs, place = call(
        functools.partial(owner_kernel, slots, packed),
        "owner",
        vmem(3),
        [rows, index],
        [held],
        10_000_000,
    )(asked, dense, camera)
    arrived = travel(attrs, peers, slots, packed)
    image, back = call(
        functools.partial(render_kernel, packed),
        "render",
        vmem(6) + smem(1),
        [shape(3, tiles, WIDE), rows],
        [
            pltpu.VMEM((3, tiles, WIDE), f32),
            pltpu.SemaphoreType.DMA,
            held,
            held,
            pltpu.VMEM((2, 48 * tiles, 128), f32),
            pltpu.VMEM((2, 16 * tiles, 128), f32),
            pltpu.VMEM((WIDE, WIDE), bf16),
            pltpu.VMEM((WIDE, WIDE), bf16),
            pltpu.VMEM((WIDE, 32), bf16),
            pltpu.VMEM((16, WIDE), bf16),
        ],
        100_000_000,
        far(1) + vmem(1),
    )(arrived, member, inverse, light, turned, centre, plan)
    returned = travel(back, peers, slots, packed)
    (grad_params,) = call(
        functools.partial(return_kernel, slots, packed),
        "return",
        vmem(4),
        [shape(width, count)],
        [
            held,
            held,
            pltpu.VMEM((2, width * blocks, 128), f32),
            pltpu.VMEM((width, count), f32),
            pltpu.SemaphoreType.DMA((2 * -(-width // 8),)),
        ],
        10_000_000,
        far(1),
    )(returned, place, dense, camera)
    return (jnp.swapaxes(image, 0, 1), grad_params)


def solution(mesh):
    return jax.shard_map(
        on_device,
        mesh=mesh,
        in_specs=(
            P(None, ("groups", "gs")),
            P(("groups", "gs"), None),
            P(("groups", "gs"), None),
            P(("groups", "gs")),
            P(("groups", "gs")),
            P(None, "groups"),
            P(("groups", "gs"), None, None),
        ),
        out_specs=(P(("groups", "gs"), None, None), P(None, ("groups", "gs"))),
        check_vma=False,
    )
```

```python
import functools

import jax
import jax.numpy as jnp
from jax import lax
from jax.experimental import pallas as pl
from jax.experimental.pallas import tpu as pltpu
from jax.sharding import PartitionSpec as P

f32, bf16, i32 = jnp.float32, jnp.bfloat16, jnp.int32

WIDE = 256
ATTRS = 9
SIDE = 16
ACROSS = 240
SCALE = 1920.0
LOG2E = 1.4426950408889634
GROUP = 4
FAR = -1.0e9

sh_c0 = 0.28209479177387814
sh_c1 = 0.4886025119029199
sh_c2 = (
    1.0925484305920792,
    -1.0925484305920792,
    0.31539156525252005,
    -1.0925484305920792,
    0.5462742152960396,
)
sh_c3 = (
    -0.5900435899266435,
    2.890611442640554,
    -0.4570457994644658,
    0.3731763325901154,
    -0.4570457994644658,
    1.445305721320277,
    -0.5900435899266435,
)


def outline(table, shift):
    xpos = table[0] - shift[0]
    ypos = table[1] - shift[1]
    zpos = table[2] - shift[2]
    scales = [jnp.exp(table[3 + k]) for k in range(3)]
    quat = table[6:10]
    norm = 1.0 / jnp.sqrt(sum(part * part for part in quat))
    qw, qx, qy, qz = (part * norm for part in quat)
    rot = [
        [1 - 2 * (qy * qy + qz * qz), 2 * (qx * qy - qw * qz), 2 * (qx * qz + qw * qy)],
        [2 * (qx * qy + qw * qz), 1 - 2 * (qx * qx + qz * qz), 2 * (qy * qz - qw * qx)],
        [2 * (qx * qz - qw * qy), 2 * (qy * qz + qw * qx), 1 - 2 * (qx * qx + qy * qy)],
    ]
    inverse_z = 1.0 / zpos
    mean_u = xpos * inverse_z
    mean_v = ypos * inverse_z
    stretch = [scale * inverse_z for scale in scales]
    first = [(rot[0][k] - mean_u * rot[2][k]) * stretch[k] for k in range(3)]
    second = [(rot[1][k] - mean_v * rot[2][k]) * stretch[k] for k in range(3)]
    cov_a = first[0] * first[0] + first[1] * first[1] + first[2] * first[2] + 8e-08
    cov_b = first[0] * second[0] + first[1] * second[1] + first[2] * second[2]
    cov_c = second[0] * second[0] + second[1] * second[1] + second[2] * second[2] + 8e-08
    over_det = 1.0 / (cov_a * cov_c - cov_b * cov_b)
    opacity = 1.0 / (1.0 + jnp.exp(-table[10]))
    return [mean_u, mean_v, cov_c * over_det, -cov_b * over_det, cov_a * over_det, opacity]


def tints(place, coefs, shift):
    xpos = place[0] - shift[0]
    ypos = place[1] - shift[1]
    zpos = place[2] - shift[2]
    over_length = 1.0 / jnp.sqrt(xpos * xpos + ypos * ypos + zpos * zpos)
    dx, dy, dz = (xpos * over_length, ypos * over_length, zpos * over_length)
    xx, yy, zz = (dx * dx, dy * dy, dz * dz)
    basis = [
        -sh_c1 * dy,
        sh_c1 * dz,
        -sh_c1 * dx,
        sh_c2[0] * dx * dy,
        sh_c2[1] * dy * dz,
        sh_c2[2] * (2 * zz - xx - yy),
        sh_c2[3] * dx * dz,
        sh_c2[4] * (xx - yy),
        sh_c3[0] * dy * (3 * xx - yy),
        sh_c3[1] * dx * dy * dz,
        sh_c3[2] * dy * (4 * zz - xx - yy),
        sh_c3[3] * dz * (2 * zz - 3 * xx - 3 * yy),
        sh_c3[4] * dx * (4 * zz - xx - yy),
        sh_c3[5] * dz * (xx - yy),
        sh_c3[6] * dx * (xx - 3 * yy),
    ]
    colors = []
    for k in range(3):
        total = 0.5 + sh_c0 * coefs[16 * k]
        for j, part in enumerate(basis):
            total = total + part * coefs[16 * k + 1 + j]
        colors.append(jnp.maximum(total, 0.0))
    return colors


def pieces(value, count):
    out = []
    for left in range(count - 1, -1, -1):
        part = value.astype(bf16)
        out.append(part)
        if left:
            value = value - part.astype(f32)
    return out


def dot(one, other):
    return jnp.dot(one, other, preferred_element_type=f32)


def stacked(high, low, weights):
    rows = high.shape[0]
    both = dot(jnp.concatenate([high, low], axis=0), weights)
    return both[:rows] + both[rows:]


def one_hot(low_row):
    rows = lax.broadcasted_iota(i32, (WIDE, WIDE), 0).astype(f32).astype(bf16)
    low = jnp.broadcast_to(low_row.astype(f32).astype(bf16), (WIDE, WIDE))
    return jnp.where(rows == low, jnp.ones((WIDE, WIDE), bf16), jnp.zeros((WIDE, WIDE), bf16))


def get(ref, start, count, stride=1, many=WIDE):
    rows = pl.ds(start, count, stride=stride) if stride > 1 else pl.ds(start, count)
    return jnp.concatenate([ref[h, rows, :] for h in range(many // 128)], axis=1)


def put(ref, start, count, value, stride=1):
    rows = pl.ds(start, count, stride=stride) if stride > 1 else pl.ds(start, count)
    for h in range(value.shape[1] // 128):
        ref[h, rows, :] = value[:, 128 * h : 128 * h + 128]


def invert(index_ref, inverse_ref):
    blocks = index_ref.shape[0]
    high_rows = lax.broadcasted_iota(i32, (blocks, WIDE), 0)
    lanes = lax.broadcasted_iota(i32, (blocks, WIDE), 1).astype(f32)
    wide_lanes = lax.broadcasted_iota(i32, (WIDE, WIDE), 1).astype(f32)
    lows = (index_ref[...] & (WIDE - 1)).astype(f32).T.astype(bf16)
    thin = wide_lanes.astype(bf16)
    ones, zeros = jnp.ones((WIDE, WIDE), bf16), jnp.zeros((WIDE, WIDE), bf16)
    total = None
    for j in range(blocks):
        here = high_rows == lax.shift_right_logical(index_ref[j : j + 1, :], 8)
        left = jnp.concatenate([jnp.where(here, float(j), 0.0), jnp.where(here, lanes, 0.0)], axis=0)
        low = jnp.broadcast_to(lows[:, j : j + 1], (WIDE, WIDE))
        part = dot(left.astype(bf16), jnp.where(thin == low, ones, zeros))
        total = part if total is None else total + part
    found = total[:blocks] * float(WIDE) + total[blocks:]
    inverse_ref[...] = found.astype(i32)


def permute(held_ref, index_ref, fine, give):
    blocks = index_ref.shape[0]
    rows = ATTRS * blocks
    thirds = [pieces(get(held_ref, a, blocks, 8), 3)[2] for a in range(fine)]
    stack = jnp.concatenate(pieces(get(held_ref, 0, rows), 2) + thirds, axis=0)
    high_rows = lax.broadcasted_iota(i32, (blocks, WIDE), 0)
    place = lax.broadcasted_iota(i32, (8, WIDE), 0)
    for j in range(blocks):
        row = index_ref[j : j + 1, :]
        high = lax.shift_right_logical(row, 8)
        here = high_rows == high
        both = dot(stack, one_hot(row & (WIDE - 1)))
        found = both[:rows] + both[rows : 2 * rows]
        high_eight = jnp.broadcast_to(high, (8, WIDE))
        eight = found[0:8]
        for b in range(1, blocks):
            eight = jnp.where(high_eight == b, found[8 * b : 8 * b + 8], eight)

        def single(values):
            return jnp.sum(jnp.where(here, values, 0.0), axis=0, keepdims=True)

        for a in range(fine):
            start = 2 * rows + a * blocks
            eight = eight + jnp.where(place == a, single(both[start : start + blocks]), 0.0)
        give(j, eight, single(found[8 * blocks :]))


def put_travel(out_ref, blocks, packed, j, eight, ninth):
    for h in range(2):
        half = slice(128 * h, 128 * h + 128)
        if packed:
            out_ref[18 * j + 8 * h : 18 * j + 8 * h + 8, :] = eight[:, half]
            out_ref[18 * j + 16 + h : 18 * j + 17 + h, :] = ninth[:, half]
        else:
            out_ref[pl.ds(2 * j + h, 8, stride=2 * blocks), :] = eight[:, half]
            out_ref[16 * blocks + 2 * j + h : 16 * blocks + 2 * j + h + 1, :] = ninth[:, half]


def take_travel(in_ref, held_ref, blocks, packed):
    for j in range(blocks):
        for h in range(2):
            if packed:
                held_ref[h, 8 * j : 8 * j + 8, :] = in_ref[18 * j + 8 * h : 18 * j + 8 * h + 8, :]
                held_ref[h, 8 * blocks + j : 8 * blocks + j + 1, :] = in_ref[18 * j + 16 + h : 18 * j + 17 + h, :]
            else:
                held_ref[h, 8 * j : 8 * j + 8, :] = in_ref[pl.ds(2 * j + h, 8, stride=2 * blocks), :]
                held_ref[h, 8 * blocks + j : 8 * blocks + j + 1, :] = in_ref[
                    16 * blocks + 2 * j + h : 16 * blocks + 2 * j + h + 1, :
                ]


def spread_scalars(values, tiles):
    rows = lax.broadcasted_iota(i32, (tiles, WIDE), 0)
    out = jnp.full((tiles, WIDE), values[0], values[0].dtype)
    for t in range(1, tiles):
        out = jnp.where(rows == t, values[t], out)
    return out


def dense_kernel(params_ref, dense_ref):
    width, count = params_ref.shape
    blocks = count // WIDE
    for first in range(0, width, 8):
        rows = min(8, width - first)
        for j in range(blocks):
            value = params_ref[first : first + rows, WIDE * j : WIDE * (j + 1)]
            put(dense_ref, first * blocks + j, rows, value, blocks)


def prepare_kernel(
    member_ref,
    grad_ref,
    length_ref,
    place_ref,
    cam_ref,
    inverse_ref,
    light_ref,
    turned_ref,
    centre_ref,
    camera_ref,
    plan_ref,
    light,
):
    tiles = grad_ref.shape[1]
    across = [lax.rem(place_ref[t], ACROSS).astype(f32) for t in range(tiles)]
    down = [lax.div(place_ref[t], ACROSS).astype(f32) for t in range(tiles)]
    centre_ref[0] = spread_scalars([(x * SIDE + SIDE / 2) / SCALE - 1.0 for x in across], tiles)
    centre_ref[1] = spread_scalars([(y * SIDE + SIDE / 2) / SCALE - 0.5625 for y in down], tiles)
    lengths = spread_scalars([length_ref[t] for t in range(tiles)], tiles)
    live = lax.broadcasted_iota(i32, (tiles, WIDE), 1) < lengths
    centre_ref[2] = jnp.where(live, 1.0, 0.0)
    views = cam_ref.shape[1]
    for axis in range(3):
        for k in range(views):
            row = axis * views + k
            camera_ref[row : row + 1, :] = jnp.broadcast_to(cam_ref[axis : axis + 1, k : k + 1], (1, WIDE))
    wide = [(length_ref[t] > WIDE // 2).astype(i32) for t in range(tiles)]
    many = sum(wide[1:], wide[0])
    first, last = jnp.int32(0), many
    for t in range(tiles):
        plan_ref[jnp.where(wide[t] > 0, first, last)] = t
        first, last = first + wide[t], last + 1 - wide[t]
    whole = lax.div(many + GROUP // 2 - 1, GROUP)
    plan_ref[tiles] = whole
    plan_ref[tiles + 1] = lax.div(many + GROUP - 1, GROUP)

    invert(member_ref, inverse_ref)

    light[...] = jnp.zeros_like(light)
    for t in range(tiles):
        high, low = pieces(jnp.concatenate([grad_ref[k, t : t + 1, :] for k in range(3)], axis=0), 2)
        light[16 * t : 16 * t + 3, :] = high.astype(f32)
        light[16 * t + 3 : 16 * t + 6, :] = low.astype(f32)
        light[16 * t + 6 : 16 * t + 9, :] = high.astype(f32)
    light_ref[...] = light[...].astype(bf16)
    for t in range(tiles):
        turned_ref[t] = light[16 * t : 16 * t + 16, :].T.astype(bf16)


def shifts(inverse, slots_per, camera_ref):
    views = camera_ref.shape[0] // 3
    view = lax.rem(lax.div(inverse, slots_per), views)
    out = []
    for axis in range(3):
        rows = [camera_ref[axis * views + k : axis * views + k + 1, :] for k in range(views)]
        value = jnp.broadcast_to(rows[0], inverse.shape)
        for k in range(1, views):
            value = jnp.where(view == k, rows[k], value)
        out.append(value)
    return out


def dense_rows(ref, count, blocks):
    return [get(ref, k * blocks, blocks) for k in range(count)]


def owner_kernel(slots_per, packed, asked_ref, dense_ref, camera_ref, attrs_ref, inverse_ref, held):
    blocks = asked_ref.shape[0]
    width = dense_ref.shape[1] // blocks
    invert(asked_ref, inverse_ref)
    shift = shifts(inverse_ref[...], slots_per, camera_ref)
    table = dense_rows(dense_ref, width, blocks)
    attrs = outline(table, shift) + tints(table[:3], table[11:], shift)
    for a in range(8):
        put(held, a, blocks, attrs[a], 8)
    put(held, 8 * blocks, blocks, attrs[8])
    permute(held, asked_ref, 2, functools.partial(put_travel, attrs_ref, blocks, packed))


def return_kernel(slots_per, packed, back_ref, inverse_ref, dense_ref, camera_ref, out_far, held, flat, grads, out_ref, sent):
    blocks = inverse_ref.shape[0]
    width = dense_ref.shape[1] // blocks
    half = blocks // 2
    take_travel(back_ref, held, blocks, packed)

    sends = []

    def send_rows(first, near):
        count = min(8, width - first)
        for j in range(near, near + half):
            value = get(grads, first * blocks + j, count, blocks)
            out_ref[first : first + count, WIDE * j : WIDE * (j + 1)] = value
        part = (pl.ds(first, count), pl.ds(WIDE * near, WIDE * half))
        sends.append(pltpu.make_async_copy(out_ref.at[part], out_far.at[part], sent.at[len(sends)]))
        sends[-1].start()

    def finish(near):
        table = [get(dense_ref, k * blocks + near, half) for k in range(width)]
        given = [get(flat, k * blocks + near, half) for k in range(ATTRS)]
        shift = shifts(inverse_ref[near : near + half, :], slots_per, camera_ref)
        _, back = jax.vjp(lambda place, coefs: tints(place, coefs, shift), table[:3], table[11:])
        drift, slopes = back(given[6:])
        for k in range(11, width):
            put(grads, k * blocks + near, half, slopes[k - 11])
        for first in range(16, width, 8):
            send_rows(first, near)
        _, back = jax.vjp(lambda rows: outline(rows, shift), table[:11])
        (slopes,) = back(given[:6])
        for k in range(11):
            put(grads, k * blocks + near, half, slopes[k] + drift[k] if k < 3 else slopes[k])
        for first in range(0, 16, 8):
            send_rows(first, near)

    def give(j, eight, ninth):
        put(flat, j, 8, eight, blocks)
        put(flat, 8 * blocks + j, 1, ninth)
        if (j + 1) % half == 0:
            finish(j + 1 - half)

    permute(held, inverse_ref, 0, give)
    for send in sends:
        send.wait()


def offsets(index):
    column = lax.rem(index, SIDE).astype(f32) - (SIDE - 1) / 2
    row = lax.div(index, SIDE).astype(f32) - (SIDE - 1) / 2
    return column, row


def pick(index, choices):
    out = jnp.zeros(index.shape, f32)
    for k, choice in enumerate(choices):
        out = jnp.where(index == k, choice, out)
    return out


def render_kernel(
    packed,
    arrived_ref,
    member_ref,
    inverse_ref,
    light_ref,
    turned_ref,
    centre_ref,
    plan_ref,
    image_ref,
    back_ref,
    image,
    sent,
    held,
    flat,
    coefs,
    sums,
    upper,
    lower,
    monomials,
    moments,
):
    tiles = member_ref.shape[0]
    blocks = tiles
    take_travel(arrived_ref, held, blocks, packed)

    def give(j, eight, ninth):
        put(flat, j, 8, eight, blocks)
        put(flat, 8 * blocks + j, 1, ninth)

    permute(held, member_ref, 2, give)

    mu, nu, con_a, con_b, con_c, opacity, *colors = dense_rows(flat, ATTRS, blocks)
    centre_u, centre_v, live = (centre_ref[k] for k in range(3))
    live = live > 0.0
    m = (mu - centre_u) * SCALE
    n = (nu - centre_v) * SCALE
    unit = LOG2E / (SCALE * SCALE)
    a = con_a * (-0.5 * unit)
    b = con_b * -unit
    c = con_c * (-0.5 * unit)
    lift = -2.0 * a * m - b * n
    tilt = -2.0 * c * n - b * m
    rest = -0.5 * (lift * m + tilt * n) + jnp.log2(opacity)
    terms = [a, b, c, lift, tilt]
    terms = [jnp.where(live, term, 0.0) for term in terms] + [jnp.where(live, rest, FAR)]
    for row in [*range(18, 32), *range(41, 48)]:
        put(coefs, row * tiles, tiles, jnp.zeros((tiles, WIDE), f32))
    for k, term in enumerate(terms):
        for s, part in enumerate(pieces(term, 3)):
            row = 6 * s + k
            put(coefs, row * tiles, tiles, part.astype(f32))
    for k, color in enumerate(colors):
        high, low = (part.astype(f32) for part in pieces(color, 2))
        for row, part in ((32 + k, high), (35 + k, high), (38 + k, low)):
            put(coefs, row * tiles, tiles, part)

    row_index = lax.broadcasted_iota(i32, (WIDE, WIDE), 0)
    lane_index = lax.broadcasted_iota(i32, (WIDE, WIDE), 1)
    upper[...] = jnp.where(row_index < lane_index, 1.0, 0.0).astype(bf16)
    lower[...] = jnp.where(row_index > lane_index, 1.0, 0.0).astype(bf16)
    column, row = offsets(lax.broadcasted_iota(i32, (WIDE, 32), 0))
    which = lax.broadcasted_iota(i32, (WIDE, 32), 1)
    which = jnp.where(which < 18, lax.rem(which, 6), 6)
    one = jnp.ones((WIDE, 32), f32)
    monomials[...] = pick(
        which, [column * column, column * row, row * row, column, row, one]
    ).astype(bf16)
    column, row = offsets(lax.broadcasted_iota(i32, (16, WIDE), 1))
    which = lax.broadcasted_iota(i32, (16, WIDE), 0)
    one = jnp.ones((16, WIDE), f32)
    moments[...] = pick(
        which, [column * column, column * row, row * row, column, row, one]
    ).astype(bf16)
    sums[...] = jnp.zeros_like(sums)

    def some_tiles(turn, many):
        ts = [plan_ref[GROUP * turn + k] for k in range(GROUP)]
        coef = [get(coefs, t, 32, tiles, n).astype(bf16) for t, n in zip(ts, many)]
        color = [get(coefs, t + 32 * tiles, 16, tiles, n).astype(bf16) for t, n in zip(ts, many)]
        alpha = [jnp.minimum(jnp.exp2(dot(monomials[...], x)), 0.99) for x in coef]
        parts = [pieces(jnp.log2(1.0 - x), 2) for x in alpha]
        through = [jnp.exp2(stacked(high, low, upper[:n, :n])) for (high, low), n in zip(parts, many)]
        weight = [x * y for x, y in zip(alpha, through)]
        parts = [pieces(x, 2) for x in weight]
        for t, x, (high, low) in zip(ts, color, parts):
            turned = x.astype(f32).T.astype(bf16)
            picture = stacked(high, low, turned).T
            for channel in range(3):
                image[channel, pl.ds(t, 1), :] = picture[channel : channel + 1] + picture[channel + 6 : channel + 7]
            rows = pl.ds(pl.multiple_of(16 * t, 16), 16)
            lit = light_ref[rows, :]
            tint = dot(jnp.concatenate([lit, lit], axis=1), jnp.concatenate([high, low], axis=0))
            put(sums, pl.multiple_of(16 * t + 8, 8), 8, tint[0:8] + pltpu.roll(tint[0:8], 5, 0))
        pulled = [dot(turned_ref[t], x) * y for t, x, y in zip(ts, color, weight)]
        parts = [pieces(x, 2) for x in pulled]
        behind = [stacked(high, low, lower[:n, :n]) for (high, low), n in zip(parts, many)]
        for k, t in enumerate(ts):
            slope = pulled[k] - behind[k] * (alpha[k] / (1.0 - alpha[k]))
            high, low = pieces(jnp.where(alpha[k] < 0.99, slope, 0.0), 2)
            moment = dot(jnp.concatenate([moments[...]] * 2, axis=1), jnp.concatenate([high, low], axis=0))
            put(sums, pl.multiple_of(16 * t, 16), 8, moment[0:8])

    def turns(first, last, *many):
        def one_turn(turn, carry):
            some_tiles(turn, many)
            return carry

        lax.fori_loop(first, last, one_turn, 0)

    wide, mixed = plan_ref[tiles], plan_ref[tiles + 1]
    turns(0, wide, *[WIDE] * GROUP)
    turns(wide, mixed, *[WIDE] * (GROUP // 2), *[WIDE // 2] * (GROUP // 2))
    turns(mixed, tiles // GROUP, *[WIDE // 2] * GROUP)
    send = pltpu.make_async_copy(image, image_ref, sent)
    send.start()

    m_xx, m_xy, m_yy, m_x, m_y, m_one = [get(sums, k, tiles, 16) for k in range(6)]
    d_x = m_x - m * m_one
    d_y = m_y - n * m_one
    d_xx = m_xx - m * (m_x + d_x)
    d_xy = m_xy - m * m_y - n * d_x
    d_yy = m_yy - n * (m_y + d_y)
    shrink = 1.0 / SCALE
    grads = [
        (con_a * d_x + con_b * d_y) * shrink,
        (con_c * d_y + con_b * d_x) * shrink,
        d_xx * (-0.5 * shrink * shrink),
        d_xy * (-shrink * shrink),
        d_yy * (-0.5 * shrink * shrink),
        m_one / opacity,
        *[get(sums, 8 + k, tiles, 16) for k in range(3)],
    ]
    for k in range(8):
        put(held, k, blocks, grads[k], 8)
    put(held, 8 * blocks, blocks, grads[8])
    permute(held, inverse_ref, 0, functools.partial(put_travel, back_ref, blocks, packed))
    send.wait()


def vmem(count):
    return [pl.BlockSpec(memory_space=pltpu.VMEM)] * count


def far(count):
    return [pl.BlockSpec(memory_space=pltpu.HBM)] * count


def smem(count):
    return [pl.BlockSpec(memory_space=pltpu.SMEM)] * count


def shape(*dims, dtype=f32):
    return jax.ShapeDtypeStruct(dims, dtype)


def call(kernel, name, ins, outs, scratch, cycles, places=None):
    return pl.pallas_call(
        kernel,
        out_shape=outs,
        in_specs=ins,
        out_specs=places or vmem(len(outs)),
        scratch_shapes=scratch,
        name=name,
        compiler_params=pltpu.CompilerParams(vmem_limit_bytes=48 * 1024 * 1024),
        cost_estimate=pl.CostEstimate(flops=cycles, bytes_accessed=4_000_000, transcendentals=0),
    )


def travel(rows, peers, slots, packed):
    total = rows.shape[0]
    if packed:
        parts = rows.reshape(peers, 1, -1)
    else:
        parts = jnp.swapaxes(rows.reshape(ATTRS, peers, slots), 0, 1)
    parts = lax.all_to_all(parts, "gs", split_axis=0, concat_axis=0, tiled=True)
    if not packed:
        parts = jnp.swapaxes(parts, 0, 1)
    return parts.reshape(total, 128)


def on_device(params, requests, member, tile_len, tile_pos, cam_shift, pixel_grad):
    peers, slots = requests.shape
    width, count = params.shape
    tiles = member.shape[0]
    blocks = count // WIDE
    packed = slots % WIDE == 0
    held = pltpu.VMEM((2, ATTRS * blocks, 128), f32)
    rows = shape(18 * blocks, 128)
    index = shape(blocks, WIDE, dtype=i32)

    asked = lax.all_to_all(requests, "gs", split_axis=0, concat_axis=0, tiled=True)
    asked = asked.reshape(blocks, WIDE)
    (dense,) = call(dense_kernel, "dense", vmem(1), [shape(2, width * blocks, 128)], [], 1_000_000)(params)
    inverse, light, turned, centre, camera, plan = call(
        prepare_kernel,
        "prepare",
        vmem(2) + smem(2) + vmem(1),
        [
            index,
            shape(16 * tiles, WIDE, dtype=bf16),
            shape(tiles, WIDE, 16, dtype=bf16),
            shape(3, tiles, WIDE),
            shape(3 * cam_shift.shape[1], WIDE),
            shape(tiles + 2, dtype=i32),
        ],
        [
            pltpu.VMEM((16 * tiles, WIDE), f32),
        ],
        10_000_000,
        vmem(5) + smem(1),
    )(member, jnp.swapaxes(pixel_grad, 0, 1), tile_len, tile_pos, cam_shift)
    attrs, place = call(
        functools.partial(owner_kernel, slots, packed),
        "owner",
        vmem(3),
        [rows, index],
        [held],
        10_000_000,
    )(asked, dense, camera)
    arrived = travel(attrs, peers, slots, packed)
    image, back = call(
        functools.partial(render_kernel, packed),
        "render",
        vmem(6) + smem(1),
        [shape(3, tiles, WIDE), rows],
        [
            pltpu.VMEM((3, tiles, WIDE), f32),
            pltpu.SemaphoreType.DMA,
            held,
            held,
            pltpu.VMEM((2, 48 * tiles, 128), f32),
            pltpu.VMEM((2, 16 * tiles, 128), f32),
            pltpu.VMEM((WIDE, WIDE), bf16),
            pltpu.VMEM((WIDE, WIDE), bf16),
            pltpu.VMEM((WIDE, 32), bf16),
            pltpu.VMEM((16, WIDE), bf16),
        ],
        100_000_000,
        far(1) + vmem(1),
    )(arrived, member, inverse, light, turned, centre, plan)
    returned = travel(back, peers, slots, packed)
    (grad_params,) = call(
        functools.partial(return_kernel, slots, packed),
        "return",
        vmem(4),
        [shape(width, count)],
        [
            held,
            held,
            pltpu.VMEM((2, width * blocks, 128), f32),
            pltpu.VMEM((width, count), f32),
            pltpu.SemaphoreType.DMA((2 * -(-width // 8),)),
        ],
        10_000_000,
        far(1),
    )(returned, place, dense, camera)
    return (jnp.swapaxes(image, 0, 1), grad_params)


def solution(mesh):
    return jax.shard_map(
        on_device,
        mesh=mesh,
        in_specs=(
            P(None, ("groups", "gs")),
            P(("groups", "gs"), None),
            P(("groups", "gs"), None),
            P(("groups", "gs")),
            P(("groups", "gs")),
            P(None, "groups"),
            P(("groups", "gs"), None, None),
        ),
        out_specs=(P(("groups", "gs"), None, None), P(None, ("groups", "gs"))),
        check_vma=False,
    )
```

```python
import functools

import jax
import jax.numpy as jnp
from jax import lax
from jax.experimental import pallas as pl
from jax.experimental.pallas import tpu as pltpu
from jax.sharding import PartitionSpec as P

f32, bf16, i32 = jnp.float32, jnp.bfloat16, jnp.int32

WIDE = 256
ATTRS = 9
SIDE = 16
ACROSS = 240
SCALE = 1920.0
LOG2E = 1.4426950408889634
GROUP = 4
FAR = -1.0e9

sh_c0 = 0.28209479177387814
sh_c1 = 0.4886025119029199
sh_c2 = (
    1.0925484305920792,
    -1.0925484305920792,
    0.31539156525252005,
    -1.0925484305920792,
    0.5462742152960396,
)
sh_c3 = (
    -0.5900435899266435,
    2.890611442640554,
    -0.4570457994644658,
    0.3731763325901154,
    -0.4570457994644658,
    1.445305721320277,
    -0.5900435899266435,
)


def outline(table, shift):
    xpos = table[0] - shift[0]
    ypos = table[1] - shift[1]
    zpos = table[2] - shift[2]
    scales = [jnp.exp(table[3 + k]) for k in range(3)]
    quat = table[6:10]
    norm = 1.0 / jnp.sqrt(sum(part * part for part in quat))
    qw, qx, qy, qz = (part * norm for part in quat)
    rot = [
        [1 - 2 * (qy * qy + qz * qz), 2 * (qx * qy - qw * qz), 2 * (qx * qz + qw * qy)],
        [2 * (qx * qy + qw * qz), 1 - 2 * (qx * qx + qz * qz), 2 * (qy * qz - qw * qx)],
        [2 * (qx * qz - qw * qy), 2 * (qy * qz + qw * qx), 1 - 2 * (qx * qx + qy * qy)],
    ]
    inverse_z = 1.0 / zpos
    mean_u = xpos * inverse_z
    mean_v = ypos * inverse_z
    stretch = [scale * inverse_z for scale in scales]
    first = [(rot[0][k] - mean_u * rot[2][k]) * stretch[k] for k in range(3)]
    second = [(rot[1][k] - mean_v * rot[2][k]) * stretch[k] for k in range(3)]
    cov_a = first[0] * first[0] + first[1] * first[1] + first[2] * first[2] + 8e-08
    cov_b = first[0] * second[0] + first[1] * second[1] + first[2] * second[2]
    cov_c = second[0] * second[0] + second[1] * second[1] + second[2] * second[2] + 8e-08
    over_det = 1.0 / (cov_a * cov_c - cov_b * cov_b)
    opacity = 1.0 / (1.0 + jnp.exp(-table[10]))
    return [mean_u, mean_v, cov_c * over_det, -cov_b * over_det, cov_a * over_det, opacity]


def tints(place, coefs, shift):
    xpos = place[0] - shift[0]
    ypos = place[1] - shift[1]
    zpos = place[2] - shift[2]
    over_length = 1.0 / jnp.sqrt(xpos * xpos + ypos * ypos + zpos * zpos)
    dx, dy, dz = (xpos * over_length, ypos * over_length, zpos * over_length)
    xx, yy, zz = (dx * dx, dy * dy, dz * dz)
    basis = [
        -sh_c1 * dy,
        sh_c1 * dz,
        -sh_c1 * dx,
        sh_c2[0] * dx * dy,
        sh_c2[1] * dy * dz,
        sh_c2[2] * (2 * zz - xx - yy),
        sh_c2[3] * dx * dz,
        sh_c2[4] * (xx - yy),
        sh_c3[0] * dy * (3 * xx - yy),
        sh_c3[1] * dx * dy * dz,
        sh_c3[2] * dy * (4 * zz - xx - yy),
        sh_c3[3] * dz * (2 * zz - 3 * xx - 3 * yy),
        sh_c3[4] * dx * (4 * zz - xx - yy),
        sh_c3[5] * dz * (xx - yy),
        sh_c3[6] * dx * (xx - 3 * yy),
    ]
    colors = []
    for k in range(3):
        total = 0.5 + sh_c0 * coefs[16 * k]
        for j, part in enumerate(basis):
            total = total + part * coefs[16 * k + 1 + j]
        colors.append(jnp.maximum(total, 0.0))
    return colors


def pieces(value, count):
    out = []
    for left in range(count - 1, -1, -1):
        part = value.astype(bf16)
        out.append(part)
        if left:
            value = value - part.astype(f32)
    return out


def dot(one, other):
    return jnp.dot(one, other, preferred_element_type=f32)


def stacked(high, low, weights):
    rows = high.shape[0]
    both = dot(jnp.concatenate([high, low], axis=0), weights)
    return both[:rows] + both[rows:]


def one_hot(low_row):
    rows = lax.broadcasted_iota(i32, (WIDE, WIDE), 0).astype(f32).astype(bf16)
    low = jnp.broadcast_to(low_row.astype(f32).astype(bf16), (WIDE, WIDE))
    return jnp.where(rows == low, jnp.ones((WIDE, WIDE), bf16), jnp.zeros((WIDE, WIDE), bf16))


def get(ref, start, count, stride=1, many=WIDE):
    rows = pl.ds(start, count, stride=stride) if stride > 1 else pl.ds(start, count)
    return jnp.concatenate([ref[h, rows, :] for h in range(many // 128)], axis=1)


def put(ref, start, count, value, stride=1):
    rows = pl.ds(start, count, stride=stride) if stride > 1 else pl.ds(start, count)
    for h in range(value.shape[1] // 128):
        ref[h, rows, :] = value[:, 128 * h : 128 * h + 128]


def invert(index_ref, inverse_ref):
    blocks = index_ref.shape[0]
    high_rows = lax.broadcasted_iota(i32, (blocks, WIDE), 0)
    lanes = lax.broadcasted_iota(i32, (blocks, WIDE), 1).astype(f32)
    wide_lanes = lax.broadcasted_iota(i32, (WIDE, WIDE), 1).astype(f32)
    lows = (index_ref[...] & (WIDE - 1)).astype(f32).T.astype(bf16)
    thin = wide_lanes.astype(bf16)
    ones, zeros = jnp.ones((WIDE, WIDE), bf16), jnp.zeros((WIDE, WIDE), bf16)
    total = None
    for j in range(blocks):
        here = high_rows == lax.shift_right_logical(index_ref[j : j + 1, :], 8)
        left = jnp.concatenate([jnp.where(here, float(j), 0.0), jnp.where(here, lanes, 0.0)], axis=0)
        low = jnp.broadcast_to(lows[:, j : j + 1], (WIDE, WIDE))
        part = dot(left.astype(bf16), jnp.where(thin == low, ones, zeros))
        total = part if total is None else total + part
    found = total[:blocks] * float(WIDE) + total[blocks:]
    inverse_ref[...] = found.astype(i32)


def permute(held_ref, index_ref, fine, give):
    blocks = index_ref.shape[0]
    rows = ATTRS * blocks
    thirds = [pieces(get(held_ref, a, blocks, 8), 3)[2] for a in range(fine)]
    stack = jnp.concatenate(pieces(get(held_ref, 0, rows), 2) + thirds, axis=0)
    high_rows = lax.broadcasted_iota(i32, (blocks, WIDE), 0)
    place = lax.broadcasted_iota(i32, (8, WIDE), 0)
    for j in range(blocks):
        row = index_ref[j : j + 1, :]
        high = lax.shift_right_logical(row, 8)
        here = high_rows == high
        both = dot(stack, one_hot(row & (WIDE - 1)))
        found = both[:rows] + both[rows : 2 * rows]
        high_eight = jnp.broadcast_to(high, (8, WIDE))
        eight = found[0:8]
        for b in range(1, blocks):
            eight = jnp.where(high_eight == b, found[8 * b : 8 * b + 8], eight)

        def single(values):
            return jnp.sum(jnp.where(here, values, 0.0), axis=0, keepdims=True)

        for a in range(fine):
            start = 2 * rows + a * blocks
            eight = eight + jnp.where(place == a, single(both[start : start + blocks]), 0.0)
        give(j, eight, single(found[8 * blocks :]))


def put_travel(out_ref, blocks, packed, j, eight, ninth):
    for h in range(2):
        half = slice(128 * h, 128 * h + 128)
        if packed:
            out_ref[18 * j + 8 * h : 18 * j + 8 * h + 8, :] = eight[:, half]
            out_ref[18 * j + 16 + h : 18 * j + 17 + h, :] = ninth[:, half]
        else:
            out_ref[pl.ds(2 * j + h, 8, stride=2 * blocks), :] = eight[:, half]
            out_ref[16 * blocks + 2 * j + h : 16 * blocks + 2 * j + h + 1, :] = ninth[:, half]


def take_travel(in_ref, held_ref, blocks, packed):
    for j in range(blocks):
        for h in range(2):
            if packed:
                held_ref[h, 8 * j : 8 * j + 8, :] = in_ref[18 * j + 8 * h : 18 * j + 8 * h + 8, :]
                held_ref[h, 8 * blocks + j : 8 * blocks + j + 1, :] = in_ref[18 * j + 16 + h : 18 * j + 17 + h, :]
            else:
                held_ref[h, 8 * j : 8 * j + 8, :] = in_ref[pl.ds(2 * j + h, 8, stride=2 * blocks), :]
                held_ref[h, 8 * blocks + j : 8 * blocks + j + 1, :] = in_ref[
                    16 * blocks + 2 * j + h : 16 * blocks + 2 * j + h + 1, :
                ]


def spread_scalars(values, tiles):
    rows = lax.broadcasted_iota(i32, (tiles, WIDE), 0)
    out = jnp.full((tiles, WIDE), values[0], values[0].dtype)
    for t in range(1, tiles):
        out = jnp.where(rows == t, values[t], out)
    return out


def dense_kernel(params_ref, dense_ref):
    width, count = params_ref.shape
    blocks = count // WIDE
    for first in range(0, width, 8):
        rows = min(8, width - first)
        for j in range(blocks):
            value = params_ref[first : first + rows, WIDE * j : WIDE * (j + 1)]
            put(dense_ref, first * blocks + j, rows, value, blocks)


def prepare_kernel(
    member_ref,
    grad_ref,
    length_ref,
    place_ref,
    cam_ref,
    inverse_ref,
    light_ref,
    turned_ref,
    centre_ref,
    camera_ref,
    plan_ref,
    light,
):
    tiles = grad_ref.shape[1]
    across = [lax.rem(place_ref[t], ACROSS).astype(f32) for t in range(tiles)]
    down = [lax.div(place_ref[t], ACROSS).astype(f32) for t in range(tiles)]
    centre_ref[0] = spread_scalars([(x * SIDE + SIDE / 2) / SCALE - 1.0 for x in across], tiles)
    centre_ref[1] = spread_scalars([(y * SIDE + SIDE / 2) / SCALE - 0.5625 for y in down], tiles)
    lengths = spread_scalars([length_ref[t] for t in range(tiles)], tiles)
    live = lax.broadcasted_iota(i32, (tiles, WIDE), 1) < lengths
    centre_ref[2] = jnp.where(live, 1.0, 0.0)
    views = cam_ref.shape[1]
    for axis in range(3):
        for k in range(views):
            row = axis * views + k
            camera_ref[row : row + 1, :] = jnp.broadcast_to(cam_ref[axis : axis + 1, k : k + 1], (1, WIDE))
    wide = [(length_ref[t] > WIDE // 2).astype(i32) for t in range(tiles)]
    many = sum(wide[1:], wide[0])
    first, last = jnp.int32(0), many
    for t in range(tiles):
        plan_ref[jnp.where(wide[t] > 0, first, last)] = t
        first, last = first + wide[t], last + 1 - wide[t]
    whole = lax.div(many + GROUP // 2 - 1, GROUP)
    plan_ref[tiles] = whole
    plan_ref[tiles + 1] = lax.div(many + GROUP - 1, GROUP)

    invert(member_ref, inverse_ref)

    light[...] = jnp.zeros_like(light)
    for t in range(tiles):
        high, low = pieces(jnp.concatenate([grad_ref[k, t : t + 1, :] for k in range(3)], axis=0), 2)
        light[16 * t : 16 * t + 3, :] = high.astype(f32)
        light[16 * t + 3 : 16 * t + 6, :] = low.astype(f32)
        light[16 * t + 6 : 16 * t + 9, :] = high.astype(f32)
    light_ref[...] = light[...].astype(bf16)
    for t in range(tiles):
        turned_ref[t] = light[16 * t : 16 * t + 16, :].T.astype(bf16)


def shifts(inverse, slots_per, camera_ref):
    views = camera_ref.shape[0] // 3
    view = lax.rem(lax.div(inverse, slots_per), views)
    out = []
    for axis in range(3):
        rows = [camera_ref[axis * views + k : axis * views + k + 1, :] for k in range(views)]
        value = jnp.broadcast_to(rows[0], inverse.shape)
        for k in range(1, views):
            value = jnp.where(view == k, rows[k], value)
        out.append(value)
    return out


def dense_rows(ref, count, blocks):
    return [get(ref, k * blocks, blocks) for k in range(count)]


def owner_kernel(slots_per, packed, width, asked_ref, dense_ref, camera_ref, attrs_ref, inverse_ref, held):
    blocks = asked_ref.shape[0]
    invert(asked_ref, inverse_ref)
    shift = shifts(inverse_ref[...], slots_per, camera_ref)
    table = dense_rows(dense_ref, width, blocks)
    attrs = outline(table, shift) + tints(table[:3], table[11:], shift)
    for a in range(8):
        put(held, a, blocks, attrs[a], 8)
    put(held, 8 * blocks, blocks, attrs[8])
    permute(held, asked_ref, 2, functools.partial(put_travel, attrs_ref, blocks, packed))


def return_kernel(slots_per, packed, back_ref, inverse_ref, dense_ref, camera_ref, out_far, held, flat, grads, out_ref, sent):
    blocks = inverse_ref.shape[0]
    width = out_far.shape[0]
    half = blocks // 2
    take_travel(back_ref, held, blocks, packed)

    sends = []

    def send_rows(first, near):
        count = min(8, width - first)
        for j in range(near, near + half):
            value = get(grads, first * blocks + j, count, blocks)
            out_ref[first : first + count, WIDE * j : WIDE * (j + 1)] = value
        part = (pl.ds(first, count), pl.ds(WIDE * near, WIDE * half))
        sends.append(pltpu.make_async_copy(out_ref.at[part], out_far.at[part], sent.at[len(sends)]))
        sends[-1].start()

    def finish(near):
        table = [get(dense_ref, k * blocks + near, half) for k in range(width)]
        given = [get(flat, k * blocks + near, half) for k in range(ATTRS)]
        shift = shifts(inverse_ref[near : near + half, :], slots_per, camera_ref)
        _, back = jax.vjp(lambda place, coefs: tints(place, coefs, shift), table[:3], table[11:])
        drift, slopes = back(given[6:])
        for k in range(11, width):
            put(grads, k * blocks + near, half, slopes[k - 11])
        for first in range(16, width, 8):
            send_rows(first, near)
        _, back = jax.vjp(lambda rows: outline(rows, shift), table[:11])
        (slopes,) = back(given[:6])
        for k in range(11):
            put(grads, k * blocks + near, half, slopes[k] + drift[k] if k < 3 else slopes[k])
        for first in range(0, 16, 8):
            send_rows(first, near)

    def give(j, eight, ninth):
        put(flat, j, 8, eight, blocks)
        put(flat, 8 * blocks + j, 1, ninth)
        if (j + 1) % half == 0:
            finish(j + 1 - half)

    permute(held, inverse_ref, 0, give)
    for send in sends:
        send.wait()


def offsets(index):
    column = lax.rem(index, SIDE).astype(f32) - (SIDE - 1) / 2
    row = lax.div(index, SIDE).astype(f32) - (SIDE - 1) / 2
    return column, row


def pick(index, choices):
    out = jnp.zeros(index.shape, f32)
    for k, choice in enumerate(choices):
        out = jnp.where(index == k, choice, out)
    return out


def render_kernel(
    packed,
    arrived_ref,
    member_ref,
    inverse_ref,
    light_ref,
    turned_ref,
    centre_ref,
    plan_ref,
    image_ref,
    back_ref,
    image,
    sent,
    held,
    flat,
    coefs,
    sums,
    upper,
    lower,
    monomials,
    moments,
):
    tiles = member_ref.shape[0]
    blocks = tiles
    take_travel(arrived_ref, held, blocks, packed)

    def give(j, eight, ninth):
        put(flat, j, 8, eight, blocks)
        put(flat, 8 * blocks + j, 1, ninth)

    permute(held, member_ref, 2, give)

    mu, nu, con_a, con_b, con_c, opacity, *colors = dense_rows(flat, ATTRS, blocks)
    centre_u, centre_v, live = (centre_ref[k] for k in range(3))
    live = live > 0.0
    m = (mu - centre_u) * SCALE
    n = (nu - centre_v) * SCALE
    unit = LOG2E / (SCALE * SCALE)
    a = con_a * (-0.5 * unit)
    b = con_b * -unit
    c = con_c * (-0.5 * unit)
    lift = -2.0 * a * m - b * n
    tilt = -2.0 * c * n - b * m
    rest = -0.5 * (lift * m + tilt * n) + jnp.log2(opacity)
    terms = [a, b, c, lift, tilt]
    terms = [jnp.where(live, term, 0.0) for term in terms] + [jnp.where(live, rest, FAR)]
    for row in [*range(18, 32), *range(41, 48)]:
        put(coefs, row * tiles, tiles, jnp.zeros((tiles, WIDE), f32))
    for k, term in enumerate(terms):
        for s, part in enumerate(pieces(term, 3)):
            row = 6 * s + k
            put(coefs, row * tiles, tiles, part.astype(f32))
    for k, color in enumerate(colors):
        high, low = (part.astype(f32) for part in pieces(color, 2))
        for row, part in ((32 + k, high), (35 + k, high), (38 + k, low)):
            put(coefs, row * tiles, tiles, part)

    row_index = lax.broadcasted_iota(i32, (WIDE, WIDE), 0)
    lane_index = lax.broadcasted_iota(i32, (WIDE, WIDE), 1)
    upper[...] = jnp.where(row_index < lane_index, 1.0, 0.0).astype(bf16)
    lower[...] = jnp.where(row_index > lane_index, 1.0, 0.0).astype(bf16)
    column, row = offsets(lax.broadcasted_iota(i32, (WIDE, 32), 0))
    which = lax.broadcasted_iota(i32, (WIDE, 32), 1)
    which = jnp.where(which < 18, lax.rem(which, 6), 6)
    one = jnp.ones((WIDE, 32), f32)
    monomials[...] = pick(
        which, [column * column, column * row, row * row, column, row, one]
    ).astype(bf16)
    column, row = offsets(lax.broadcasted_iota(i32, (16, WIDE), 1))
    which = lax.broadcasted_iota(i32, (16, WIDE), 0)
    one = jnp.ones((16, WIDE), f32)
    moments[...] = pick(
        which, [column * column, column * row, row * row, column, row, one]
    ).astype(bf16)
    sums[...] = jnp.zeros_like(sums)

    def some_tiles(turn, many):
        ts = [plan_ref[GROUP * turn + k] for k in range(GROUP)]
        coef = [get(coefs, t, 32, tiles, n).astype(bf16) for t, n in zip(ts, many)]
        color = [get(coefs, t + 32 * tiles, 16, tiles, n).astype(bf16) for t, n in zip(ts, many)]
        alpha = [jnp.minimum(jnp.exp2(dot(monomials[...], x)), 0.99) for x in coef]
        parts = [pieces(jnp.log2(1.0 - x), 2) for x in alpha]
        through = [jnp.exp2(stacked(high, low, upper[:n, :n])) for (high, low), n in zip(parts, many)]
        weight = [x * y for x, y in zip(alpha, through)]
        parts = [pieces(x, 2) for x in weight]
        for t, x, (high, low) in zip(ts, color, parts):
            turned = x.astype(f32).T.astype(bf16)
            picture = stacked(high, low, turned).T
            for channel in range(3):
                image[channel, pl.ds(t, 1), :] = picture[channel : channel + 1] + picture[channel + 6 : channel + 7]
            rows = pl.ds(pl.multiple_of(16 * t, 16), 16)
            lit = light_ref[rows, :]
            tint = dot(jnp.concatenate([lit, lit], axis=1), jnp.concatenate([high, low], axis=0))
            put(sums, pl.multiple_of(16 * t + 8, 8), 8, tint[0:8] + pltpu.roll(tint[0:8], 5, 0))
        pulled = [dot(turned_ref[t], x) * y for t, x, y in zip(ts, color, weight)]
        parts = [pieces(x, 2) for x in pulled]
        behind = [stacked(high, low, lower[:n, :n]) for (high, low), n in zip(parts, many)]
        for k, t in enumerate(ts):
            slope = pulled[k] - behind[k] * (alpha[k] / (1.0 - alpha[k]))
            high, low = pieces(jnp.where(alpha[k] < 0.99, slope, 0.0), 2)
            moment = dot(jnp.concatenate([moments[...]] * 2, axis=1), jnp.concatenate([high, low], axis=0))
            put(sums, pl.multiple_of(16 * t, 16), 8, moment[0:8])

    def turns(first, last, *many):
        def one_turn(turn, carry):
            some_tiles(turn, many)
            return carry

        lax.fori_loop(first, last, one_turn, 0)

    wide, mixed = plan_ref[tiles], plan_ref[tiles + 1]
    turns(0, wide, *[WIDE] * GROUP)
    turns(wide, mixed, *[WIDE] * (GROUP // 2), *[WIDE // 2] * (GROUP // 2))
    turns(mixed, tiles // GROUP, *[WIDE // 2] * GROUP)
    send = pltpu.make_async_copy(image.at[:, pl.ds(0, tiles), :], image_ref, sent)
    send.start()

    m_xx, m_xy, m_yy, m_x, m_y, m_one = [get(sums, k, tiles, 16) for k in range(6)]
    d_x = m_x - m * m_one
    d_y = m_y - n * m_one
    d_xx = m_xx - m * (m_x + d_x)
    d_xy = m_xy - m * m_y - n * d_x
    d_yy = m_yy - n * (m_y + d_y)
    shrink = 1.0 / SCALE
    grads = [
        (con_a * d_x + con_b * d_y) * shrink,
        (con_c * d_y + con_b * d_x) * shrink,
        d_xx * (-0.5 * shrink * shrink),
        d_xy * (-shrink * shrink),
        d_yy * (-0.5 * shrink * shrink),
        m_one / opacity,
        *[get(sums, 8 + k, tiles, 16) for k in range(3)],
    ]
    for k in range(8):
        put(held, k, blocks, grads[k], 8)
    put(held, 8 * blocks, blocks, grads[8])
    permute(held, inverse_ref, 0, functools.partial(put_travel, back_ref, blocks, packed))
    send.wait()


def vmem(count):
    return [pl.BlockSpec(memory_space=pltpu.VMEM)] * count


def far(count):
    return [pl.BlockSpec(memory_space=pltpu.HBM)] * count


def smem(count):
    return [pl.BlockSpec(memory_space=pltpu.SMEM)] * count


def shape(*dims, dtype=f32):
    return jax.ShapeDtypeStruct(dims, dtype)


def call(kernel, name, ins, outs, scratch, cycles, places=None):
    return pl.pallas_call(
        kernel,
        out_shape=outs,
        in_specs=ins,
        out_specs=places or vmem(len(outs)),
        scratch_shapes=scratch,
        name=name,
        compiler_params=pltpu.CompilerParams(vmem_limit_bytes=48 * 1024 * 1024),
        cost_estimate=pl.CostEstimate(flops=cycles, bytes_accessed=4_000_000, transcendentals=0),
    )


def travel(rows, peers, slots, packed):
    total = rows.shape[0]
    if packed:
        parts = rows.reshape(peers, 1, -1)
    else:
        parts = jnp.swapaxes(rows.reshape(ATTRS, peers, slots), 0, 1)
    parts = lax.all_to_all(parts, "gs", split_axis=0, concat_axis=0, tiled=True)
    if not packed:
        parts = jnp.swapaxes(parts, 0, 1)
    return parts.reshape(total, 128)


def on_device(params, requests, member, tile_len, tile_pos, cam_shift, pixel_grad):
    peers, slots = requests.shape
    width, count = params.shape
    tall = -(-width // 8) * 8
    tiles = member.shape[0]
    blocks = count // WIDE
    packed = slots % WIDE == 0
    held = pltpu.VMEM((2, ATTRS * blocks, 128), f32)
    rows = shape(18 * blocks, 128)
    index = shape(blocks, WIDE, dtype=i32)

    asked = lax.all_to_all(requests, "gs", split_axis=0, concat_axis=0, tiled=True)
    asked = asked.reshape(blocks, WIDE)
    (dense,) = call(dense_kernel, "dense", vmem(1), [shape(2, tall * blocks, 128)], [], 1_000_000)(params)
    inverse, light, turned, centre, camera, plan = call(
        prepare_kernel,
        "prepare",
        vmem(2) + smem(2) + vmem(1),
        [
            index,
            shape(16 * tiles, WIDE, dtype=bf16),
            shape(tiles, WIDE, 16, dtype=bf16),
            shape(3, tiles, WIDE),
            shape(3 * cam_shift.shape[1], WIDE),
            shape(tiles + 2, dtype=i32),
        ],
        [
            pltpu.VMEM((16 * tiles, WIDE), f32),
        ],
        10_000_000,
        vmem(5) + smem(1),
    )(member, jnp.swapaxes(pixel_grad, 0, 1), tile_len, tile_pos, cam_shift)
    attrs, place = call(
        functools.partial(owner_kernel, slots, packed, width),
        "owner",
        vmem(3),
        [rows, index],
        [held],
        10_000_000,
    )(asked, dense, camera)
    arrived = travel(attrs, peers, slots, packed)
    image, back = call(
        functools.partial(render_kernel, packed),
        "render",
        vmem(6) + smem(1),
        [shape(3, tiles, WIDE), rows],
        [
            pltpu.VMEM((3, tiles + 8, WIDE), f32),
            pltpu.SemaphoreType.DMA,
            held,
            held,
            pltpu.VMEM((2, 48 * tiles, 128), f32),
            pltpu.VMEM((2, 16 * tiles, 128), f32),
            pltpu.VMEM((WIDE, WIDE), bf16),
            pltpu.VMEM((WIDE, WIDE), bf16),
            pltpu.VMEM((WIDE, 32), bf16),
            pltpu.VMEM((16, WIDE), bf16),
        ],
        100_000_000,
        far(1) + vmem(1),
    )(arrived, member, inverse, light, turned, centre, plan)
    returned = travel(back, peers, slots, packed)
    (grad_params,) = call(
        functools.partial(return_kernel, slots, packed),
        "return",
        vmem(4),
        [shape(width, count)],
        [
            held,
            held,
            pltpu.VMEM((2, tall * blocks, 128), f32),
            pltpu.VMEM((tall, count), f32),
            pltpu.SemaphoreType.DMA((2 * -(-width // 8),)),
        ],
        10_000_000,
        far(1),
    )(returned, place, dense, camera)
    return (jnp.swapaxes(image, 0, 1), grad_params)


def solution(mesh):
    return jax.shard_map(
        on_device,
        mesh=mesh,
        in_specs=(
            P(None, ("groups", "gs")),
            P(("groups", "gs"), None),
            P(("groups", "gs"), None),
            P(("groups", "gs")),
            P(("groups", "gs")),
            P(None, "groups"),
            P(("groups", "gs"), None, None),
        ),
        out_specs=(P(("groups", "gs"), None, None), P(None, ("groups", "gs"))),
        check_vma=False,
    )
```
